512 devices in a mesh: gx: 16 (over y_lo, x, core), gy: 32 (over z, y_hi).
Axes of the slice: x: 4, y: 8 (y_hi: 4, y_lo: 2; y = y_hi * 2 + y_lo), z: 8, core: 2. Of those that a mesh axis runs over, the one named last changes fastest.
Arguments:
- fine_nodes: bfloat16 [16, 32, 512, 128], P('gx', 'gy'), may hold values from -6 to 6
- fine_edges: int32 [16, 32, 2, 1536], P('gx', 'gy'), may hold values from 0 to 1023, as said below
- fine_live: int32 [16, 32], P('gx', 'gy'), may hold values from 512 to 1536, as said below
- fine_halo: int32 [16, 32, 4, 1], P('gx', 'gy'), may hold values from 0 to 3, as said below
- pool_map: int32 [16, 32, 512], P('gx', 'gy'), may hold values from 0 to 255, as said below
- coarse_edges: int32 [16, 32, 2, 2048], P('gx', 'gy'), may hold values from 0 to 767, as said below
- coarse_halo: int32 [16, 32, 4, 1], P('gx', 'gy'), may hold values from 0 to 1, as said below
- fine_weights: bfloat16 [5, 128, 128], replicated, may hold values from -0.5 to 0.5
- fine_bias: float32 [128], replicated, may hold values from -3 to 3
- fine_gain: float32 [128], replicated, may hold values from 0.25 to 1.75
- coarse_weights: bfloat16 [2, 5, 128, 128], replicated, may hold values from -0.5 to 0.5
- coarse_bias: float32 [2, 128], replicated, may hold values from -3 to 3
- coarse_gain: float32 [2, 128], replicated, may hold values from 0.25 to 1.75
- cotangent: bfloat16 [16, 32, 512, 128], P('gx', 'gy'), may hold values from -6 to 6
Outputs:
- fine_out: bfloat16 [16, 32, 512, 128], P('gx', 'gy')
- grad_fine_weights: float32 [5, 128, 128], replicated
- grad_fine_bias: float32 [128], replicated
- grad_fine_gain: float32 [128], replicated
- grad_coarse_weights: float32 [2, 5, 128, 128], replicated
- grad_coarse_bias: float32 [2, 128], replicated
- grad_coarse_gain: float32 [2, 128], replicated
- grad_pooled: float32 [16, 32, 256, 128], P('gx', 'gy')
The draws below stay inside these ranges and needn't reach their ends.
Inputs may be any that keep to these rules, and one draw needn't show every extreme that they name: `fine_edges`: row 0 of each device's slots names senders: below 512 a node of the device, from 512 on a row of the four halo groups; row 1 names receivers among the device's 512 nodes. `fine_live`: A multiple of 512; in every draw some device has all 1536 slots live. `fine_halo`: block numbers of the device's fine nodes; within one device and direction they differ. `pool_map`: every coarse node of a device is named by at least one of its fine nodes. `coarse_edges`: row 0 names senders: below 256 a coarse node of the device, from 256 on a row of the four coarse halo groups; row 1 names receivers among the device's 256 coarse nodes. `coarse_halo`: block numbers of the device's coarse nodes.
All inputs are finite; a program needn't handle non-finite values.
Results may differ from the reference program's by a relative error of at most 0.009.
Values may be sent and summed in bfloat16 or wider, within the bound.
No kernel may reach another device: no remote copies, remote signals or barrier semaphores. Data moves between devices by JAX's collectives and lax.ppermute only.
A program may use at most 64 MiB of HBM per device.

```python
import math
from functools import partial
import jax
import jax.numpy as jnp
from jax import lax

H = 128
BLOCK = 128
NF_DEV = 512
EDGE_BLOCK = 512
COARSE_STEPS = 2
EDGE_SLOTS = 1536
TURNS = 3
NC_DEV = 256
EC_DEV = 2048
FINE_HALO = 1
GRID_X = 16
GRID_Y = 32
FINE_NODES = 262144


def edge_draw(key, node_count, halo_count, slot_count):
    subkeys = jax.random.split(key, 4)
    grid_shape = (GRID_X, GRID_Y, slot_count)
    receivers = jax.random.randint(subkeys[0], grid_shape, 0, node_count)
    own_senders = jax.random.randint(subkeys[1], grid_shape, 0, node_count)
    remote = node_count + jax.random.randint(subkeys[2], grid_shape, 0, halo_count)
    senders = jnp.where(jax.random.randint(subkeys[3], grid_shape, 0, 4) == 0, remote, own_senders)
    return jnp.stack([senders, receivers], axis=2).astype(jnp.int32)


def distinct_blocks(key, block_count, chosen_count):
    scores = jax.random.randint(key, (GRID_X, GRID_Y, 4, block_count), 0, 1 << 20) * block_count + lax.iota(jnp.int32, block_count)
    ordered = jnp.argsort(scores, axis=-1, stable=True)
    return ordered[..., :chosen_count].astype(jnp.int32)


def draw_fine_edges(key, part):
    return edge_draw(jax.random.fold_in(key, 11), NF_DEV, 4 * FINE_HALO * BLOCK, EDGE_SLOTS)


def draw_coarse_edges(key, part):
    return edge_draw(jax.random.fold_in(key, 13), NC_DEV, 4 * BLOCK, EC_DEV)


def draw_fine_halo(key, part):
    return distinct_blocks(jax.random.fold_in(key, 15), NF_DEV // BLOCK, FINE_HALO)


def draw_coarse_halo(key, part):
    return distinct_blocks(jax.random.fold_in(key, 17), NC_DEV // BLOCK, 1)


def draw_pool_map(key, part):
    stride = NF_DEV // NC_DEV
    spots = lax.broadcasted_iota(jnp.int32, (GRID_X, GRID_Y, NF_DEV), 2)
    random_map = jax.random.randint(jax.random.fold_in(key, 19), (GRID_X, GRID_Y, NF_DEV), 0, NC_DEV)
    return jnp.where(spots % stride == 0, spots // stride, random_map).astype(jnp.int32)


def draw_fine_live(key, part):
    subkeys = jax.random.split(jax.random.fold_in(key, 21), 3)
    lowest = max(1, TURNS // 4)
    highest = max(lowest + 1, TURNS // 2 + 1)
    drawn = jax.random.randint(subkeys[0], (GRID_X, GRID_Y), lowest, highest)
    filled = jax.random.randint(subkeys[1], (GRID_X, GRID_Y), 0, 8) == 0
    chosen = jax.random.randint(subkeys[2], (), 0, GRID_X * GRID_Y)
    position = lax.broadcasted_iota(jnp.int32, (GRID_X, GRID_Y), 0) * GRID_Y + lax.broadcasted_iota(jnp.int32, (GRID_X, GRID_Y), 1)
    blocks = jnp.where(filled | (position == chosen), TURNS, drawn)
    return (blocks * EDGE_BLOCK).astype(jnp.int32)


def level_of(stream_key, dims, shards, least, largest):
    def one(dim, parts):
        heights = jax.random.uniform(jax.random.fold_in(jax.random.fold_in(stream_key, 6), dim), (parts,), jnp.float32, least / len(shards), largest / len(shards))
        return jnp.repeat(jnp.exp(heights), dims[dim] // parts).reshape((-1,) + (1,) * (len(dims) - dim - 1))

    factor_of = one(*shards[0])
    for cut in shards[1:]:
        factor_of = factor_of * one(*cut)
    return factor_of


def noise(stream_key, shape, scale, limit, cuts=(), held_as=jnp.bfloat16):
    level = level_of(stream_key, shape, cuts, -0.22, 0.18) if cuts else 1.0
    array = jax.random.normal(stream_key, shape, jnp.float32) * scale * level
    return jnp.minimum(jnp.maximum(array, -limit), limit).astype(held_as)


def setup_inputs(seed: int = 0) -> dict:
    key_list = jax.random.split(jax.random.key(seed), 15)
    return {
        "fine_nodes": noise(key_list[0], (GRID_X, GRID_Y, NF_DEV, H), 1.0, 6.0, ((0, 16), (1, 32))),
        "fine_edges": draw_fine_edges(jax.random.fold_in(key_list[14], 71), 0),
        "fine_live": draw_fine_live(jax.random.fold_in(key_list[14], 71), 0),
        "fine_halo": draw_fine_halo(jax.random.fold_in(key_list[14], 71), 0),
        "pool_map": draw_pool_map(jax.random.fold_in(key_list[14], 71), 0),
        "coarse_edges": draw_coarse_edges(jax.random.fold_in(key_list[14], 71), 0),
        "coarse_halo": draw_coarse_halo(jax.random.fold_in(key_list[14], 71), 0),
        "fine_weights": noise(key_list[7], (5, H, H), H ** -0.5, 0.5),
        "fine_bias": noise(key_list[8], (H,), 0.5, 3.0, (), jnp.float32),
        "fine_gain": jnp.clip(1.0 + 0.15 * jax.random.normal(key_list[9], (H,), jnp.float32), 0.25, 1.75),
        "coarse_weights": noise(key_list[10], (COARSE_STEPS, 5, H, H), H ** -0.5, 0.5),
        "coarse_bias": noise(key_list[11], (COARSE_STEPS, H), 0.5, 3.0, (), jnp.float32),
        "coarse_gain": jnp.clip(1.0 + 0.15 * jax.random.normal(key_list[12], (COARSE_STEPS, H), jnp.float32), 0.25, 1.75),
        "cotangent": noise(key_list[13], (GRID_X, GRID_Y, NF_DEV, H), 1.0, 6.0, ((0, 16), (1, 32))),
    }


EPSILON = 1e-05

def layer_norm(values):
    centred = values - lax.optimization_barrier(jnp.mean(values, axis=-1, keepdims=True))
    spread = lax.optimization_barrier(jnp.mean(centred * centred, axis=-1, keepdims=True))
    return centred * lax.rsqrt(spread + EPSILON)

def split_parts(values):
    high = values.astype(jnp.bfloat16)
    low = (values - high.astype(jnp.float32)).astype(jnp.bfloat16)
    return (high, low)

def contract_rows(left, right):
    high, low = split_parts(right)
    numbers = (((0,), (0,)), ((), ()))
    return lax.dot_general(left, high, numbers, preferred_element_type=jnp.float32) + lax.dot_general(left, low, numbers, preferred_element_type=jnp.float32)

def times_transpose(left, weight):
    high, low = split_parts(left)
    numbers = (((1,), (1,)), ((), ()))
    return lax.dot_general(high, weight, numbers, preferred_element_type=jnp.float32) + lax.dot_general(low, weight, numbers, preferred_element_type=jnp.float32)

def make_one_hot(pool_rows, coarse_count):
    return (pool_rows[:, None] == lax.iota(jnp.int32, coarse_count)[None, :]).astype(jnp.bfloat16)

def pick_blocks(node_rows, block_lists):
    features = node_rows.shape[-1]
    blocked = node_rows.reshape(-1, BLOCK, features)
    return blocked[block_lists].reshape(4, -1, features)

def put_blocks(returned, block_lists, row_count):
    features = returned.shape[-1]
    pieces = returned.reshape(-1, BLOCK, features)
    total = jnp.zeros((row_count // BLOCK, BLOCK, features), jnp.float32).at[block_lists.reshape(-1)].add(pieces)
    return total.reshape(row_count, features)

def slot_block(edge_list, live_slots, first_slot, block_width):
    senders = lax.dynamic_slice_in_dim(edge_list[0], first_slot, block_width)
    receivers = lax.dynamic_slice_in_dim(edge_list[1], first_slot, block_width)
    weights_live = (first_slot + lax.iota(jnp.int32, block_width) < live_slots).astype(jnp.float32)
    return (senders, receivers, weights_live)

def step_forward(node_rows, halo_rows, edge_list, live_slots, turn_count, weights, edge_bias, norm_gain, block_width):
    row_count = node_rows.shape[0]
    extended = jnp.concatenate([node_rows, halo_rows], axis=0)
    proj_send = jnp.dot(extended, weights[0], preferred_element_type=jnp.float32)
    proj_recv = jnp.dot(node_rows, weights[1], preferred_element_type=jnp.float32)

    def one_turn(turn_index, running):
        first_slot = (turn_index * block_width).astype(jnp.int32)
        senders, receivers, weights_live = slot_block(edge_list, live_slots, first_slot, block_width)
        hidden = jax.nn.silu(proj_send[senders] + proj_recv[receivers] + edge_bias).astype(jnp.bfloat16)
        message = jnp.dot(hidden, weights[2], preferred_element_type=jnp.float32) * weights_live[:, None]
        return running.at[receivers].add(message)
    summed = lax.fori_loop(0, turn_count, one_turn, jnp.zeros((row_count, proj_recv.shape[1]), jnp.float32))
    agg_low = summed.astype(jnp.bfloat16)
    node_pre = jnp.dot(node_rows, weights[3], preferred_element_type=jnp.float32) + jnp.dot(agg_low, weights[4], preferred_element_type=jnp.float32)
    output = (node_rows.astype(jnp.float32) + norm_gain * layer_norm(node_pre)).astype(jnp.bfloat16)
    return (output, (extended, proj_send, proj_recv, agg_low, node_pre))

def step_backward(upstream, node_rows, saved_state, edge_list, live_slots, turn_count, weights, edge_bias, norm_gain, block_width, want_input):
    extended, proj_send, proj_recv, agg_low, node_pre = saved_state
    row_count = node_rows.shape[0]
    features = proj_recv.shape[1]
    normed, norm_back = jax.vjp(layer_norm, node_pre)
    grad_gain = lax.optimization_barrier(jnp.sum(upstream * normed, axis=0))
    grad_pre = norm_back(upstream * norm_gain)[0]
    grad_self = contract_rows(node_rows, grad_pre)
    grad_agg_weight = contract_rows(agg_low, grad_pre)
    grad_agg = times_transpose(grad_pre, weights[4])

    def one_turn(turn_index, running):
        grad_send, grad_recv, grad_bias, grad_msg = running
        first_slot = (turn_index * block_width).astype(jnp.int32)
        senders, receivers, weights_live = slot_block(edge_list, live_slots, first_slot, block_width)
        pre_act = proj_send[senders] + proj_recv[receivers] + edge_bias
        hidden = jax.nn.silu(pre_act).astype(jnp.bfloat16)
        grad_message = grad_agg[receivers] * weights_live[:, None]
        grad_msg = grad_msg + contract_rows(hidden, grad_message)
        sigmoid = jax.nn.sigmoid(pre_act)
        grad_act = times_transpose(grad_message, weights[2]) * sigmoid * (1.0 + pre_act * (1.0 - sigmoid))
        return (grad_send.at[senders].add(grad_act), grad_recv.at[receivers].add(grad_act), grad_bias + lax.optimization_barrier(jnp.sum(grad_act, axis=0)), grad_msg)
    start_state = (jnp.zeros(proj_send.shape, jnp.float32), jnp.zeros(proj_recv.shape, jnp.float32), jnp.zeros((features,), jnp.float32), jnp.zeros((features, features), jnp.float32))
    grad_send, grad_recv, grad_bias, grad_msg = lax.fori_loop(0, turn_count, one_turn, start_state)
    grad_weights = jnp.stack([contract_rows(extended, grad_send), contract_rows(node_rows, grad_recv), grad_msg, grad_self, grad_agg_weight])
    if not want_input:
        return ((grad_weights, grad_bias, grad_gain), None, None)
    grad_ext = times_transpose(grad_send, weights[0])
    grad_nodes = upstream + times_transpose(grad_pre, weights[3]) + times_transpose(grad_recv, weights[1]) + grad_ext[:row_count]
    return ((grad_weights, grad_bias, grad_gain), grad_nodes, grad_ext[row_count:])

def from_lower(values, axis):
    length = values.shape[axis]
    zero_part = jnp.zeros_like(lax.slice_in_dim(values, 0, 1, axis=axis))
    return jnp.concatenate([zero_part, lax.slice_in_dim(values, 0, length - 1, axis=axis)], axis=axis)

def from_upper(values, axis):
    length = values.shape[axis]
    zero_part = jnp.zeros_like(lax.slice_in_dim(values, 0, 1, axis=axis))
    return jnp.concatenate([lax.slice_in_dim(values, 1, length, axis=axis), zero_part], axis=axis)

def assemble(grid_rows, block_lists):
    sends = jax.vmap(jax.vmap(pick_blocks))(grid_rows, block_lists)
    groups = [from_lower(sends[:, :, 1], 0), from_upper(sends[:, :, 0], 0), from_lower(sends[:, :, 3], 1), from_upper(sends[:, :, 2], 1)]
    return jnp.concatenate(groups, axis=2)

def assemble_back(halo_grads, block_lists, row_count):
    split = halo_grads.reshape(halo_grads.shape[:2] + (4, -1, halo_grads.shape[-1]))
    returned = jnp.stack([from_lower(split[:, :, 1], 0), from_upper(split[:, :, 0], 0), from_lower(split[:, :, 3], 1), from_upper(split[:, :, 2], 1)], axis=2)
    return jax.vmap(jax.vmap(partial(put_blocks, row_count=row_count)))(returned, block_lists)

def sum_devices(values):
    return lax.optimization_barrier(jnp.sum(values, axis=0))

def reference(fine_nodes, fine_edges, fine_live, fine_halo, pool_map, coarse_edges, coarse_halo, fine_weights, fine_bias, fine_gain, coarse_weights, coarse_bias, coarse_gain, cotangent):
    device_count = GRID_X * GRID_Y
    fine_turns = EDGE_SLOTS // EDGE_BLOCK
    coarse_slots = EC_DEV
    coarse_turns = EC_DEV // EDGE_BLOCK
    loss_scale = 1.0 / math.sqrt(FINE_NODES)

    def flatten(values):
        return values.reshape((device_count,) + values.shape[2:])

    def gridded(values):
        return values.reshape((GRID_X, GRID_Y) + values.shape[1:])
    fine_ext = flatten(assemble(fine_nodes, fine_halo))
    flat_nodes = flatten(fine_nodes)
    flat_edges = flatten(fine_edges)
    flat_live = flatten(fine_live)
    flat_pool = flatten(pool_map)
    flat_coarse_edges = flatten(coarse_edges)
    flat_cot = flatten(cotangent)

    def fine_ahead(device_item):
        node_rows, halo_rows, edge_list, live_slots = device_item
        return step_forward(node_rows, halo_rows, edge_list, live_slots, fine_turns, fine_weights, fine_bias, fine_gain, EDGE_BLOCK)[0]
    fine_mid = lax.map(fine_ahead, (flat_nodes, fine_ext, flat_edges, flat_live))

    def pooling(device_item):
        mid_rows, pool_rows = device_item
        one_hot = make_one_hot(pool_rows, NC_DEV)
        pooled_sums = lax.dot_general(one_hot, mid_rows, (((0,), (0,)), ((), ())), preferred_element_type=jnp.float32)
        counts = lax.optimization_barrier(jnp.sum(one_hot, axis=0, dtype=jnp.float32))
        return ((pooled_sums / counts[:, None]).astype(jnp.bfloat16), counts)
    current, counts = lax.map(pooling, (fine_mid, flat_pool))

    def coarse_ahead(step_index, device_item):
        node_rows, halo_rows, edge_list = device_item
        return step_forward(node_rows, halo_rows, edge_list, coarse_slots, coarse_turns, coarse_weights[step_index], coarse_bias[step_index], coarse_gain[step_index], EDGE_BLOCK)[0]
    states = []
    for step_index in range(COARSE_STEPS):
        ext_now = flatten(assemble(gridded(current), coarse_halo))
        states.append((current, ext_now))
        current = lax.map(partial(coarse_ahead, step_index), (current, ext_now, flat_coarse_edges))

    def unpooling(device_item):
        mid_rows, pool_rows, coarse_rows = device_item
        lifted = jnp.dot(make_one_hot(pool_rows, NC_DEV), coarse_rows, preferred_element_type=jnp.float32)
        return (mid_rows.astype(jnp.float32) + lifted).astype(jnp.bfloat16)
    fine_out = lax.map(unpooling, (fine_mid, flat_pool, current))

    def coarse_seed(device_item):
        cot_rows, pool_rows = device_item
        return jax.ops.segment_sum(cot_rows.astype(jnp.float32) * loss_scale, pool_rows, num_segments=NC_DEV)
    upstream = lax.map(coarse_seed, (flat_cot, flat_pool))

    def coarse_behind(step_index, device_item):
        grad_rows, node_rows, halo_rows, edge_list = device_item
        saved_state = step_forward(node_rows, halo_rows, edge_list, coarse_slots, coarse_turns, coarse_weights[step_index], coarse_bias[step_index], coarse_gain[step_index], EDGE_BLOCK)[1]
        return step_backward(grad_rows, node_rows, saved_state, edge_list, coarse_slots, coarse_turns, coarse_weights[step_index], coarse_bias[step_index], coarse_gain[step_index], EDGE_BLOCK, True)
    coarse_terms = [None] * COARSE_STEPS
    for step_index in reversed(range(COARSE_STEPS)):
        inputs_now, ext_now = states[step_index]
        step_terms, grad_nodes, grad_halo = lax.map(partial(coarse_behind, step_index), (upstream, inputs_now, ext_now, flat_coarse_edges))
        upstream = grad_nodes + flatten(assemble_back(gridded(grad_halo), coarse_halo, NC_DEV))
        coarse_terms[step_index] = jax.tree.map(sum_devices, step_terms)
    grad_pooled = gridded(upstream * math.sqrt(FINE_NODES))

    def fine_behind(device_item):
        node_rows, halo_rows, edge_list, live_slots, cot_rows, pool_rows, coarse_up, coarse_counts = device_item
        saved_state = step_forward(node_rows, halo_rows, edge_list, live_slots, fine_turns, fine_weights, fine_bias, fine_gain, EDGE_BLOCK)[1]
        direct = cot_rows.astype(jnp.float32) * loss_scale
        fine_seed = direct + (coarse_up / coarse_counts[:, None])[pool_rows]
        return step_backward(fine_seed, node_rows, saved_state, edge_list, live_slots, fine_turns, fine_weights, fine_bias, fine_gain, EDGE_BLOCK, False)[0]
    fine_terms = jax.tree.map(sum_devices, lax.map(fine_behind, (flat_nodes, fine_ext, flat_edges, flat_live, flat_cot, flat_pool, upstream, counts)))
    grad_coarse_weights = jnp.stack([entry[0] for entry in coarse_terms])
    grad_coarse_bias = jnp.stack([entry[1] for entry in coarse_terms])
    grad_coarse_gain = jnp.stack([entry[2] for entry in coarse_terms])
    return (gridded(fine_out), fine_terms[0], fine_terms[1], fine_terms[2], grad_coarse_weights, grad_coarse_bias, grad_coarse_gain, grad_pooled)
```

```python
import functools
import math

import jax
import jax.numpy as jnp
from jax import lax
from jax.experimental import pallas as pl
from jax.experimental.pallas import tpu as pltpu
from jax.sharding import PartitionSpec as P

BLOCK = 128
H = 128
COARSE_STEPS = 2
NC_DEV = 256
CHUNK = 256
GRAD_ROWS = 5 * H + 8
EPSILON = 1e-05
F32 = jnp.float32
BF16 = jnp.bfloat16


def halves(values):
    high = values.astype(BF16)
    low = (values - high.astype(F32)).astype(BF16)
    return jnp.concatenate([high, low], axis=1)


def joined(values):
    return values[:, :H] + values[:, H:]


def matmul(left, right):
    return jnp.dot(left, right, preferred_element_type=F32)


def matmul_nt(left, right):
    return lax.dot_general(left, right, (((1,), (1,)), ((), ())), preferred_element_type=F32)


def matmul_tn(left, right):
    return lax.dot_general(left, right, (((0,), (0,)), ((), ())), preferred_element_type=F32)


def twice(weight):
    return jnp.concatenate([weight, weight], axis=1)


def column_of(row):
    pieces = []
    for start in range(0, row.shape[1], 128):
        wide = jnp.broadcast_to(row[:, start : start + 128], (128, 128))
        pieces.append(wide.T)
    return pieces[0] if len(pieces) == 1 else jnp.concatenate(pieces, axis=0)


def one_hot_rows(row, width):
    spread = column_of(row)
    spread = spread - lax.broadcasted_iota(jnp.int32, spread.shape, 1)
    tiles = [jnp.where(spread == start, 1.0, 0.0).astype(BF16) for start in range(0, width, 128)]
    return jnp.concatenate(tiles, axis=1)


def one_hot_columns(row, first, count):
    shape = (count, row.shape[1])
    marks = lax.broadcasted_iota(jnp.int32, shape, 0) + first == jnp.broadcast_to(row, shape)
    return jnp.where(marks, 1.0, 0.0).astype(BF16)


def normalise(node_pre):
    centred = node_pre - jnp.mean(node_pre, axis=1, keepdims=True)
    spread = jnp.mean(centred * centred, axis=1, keepdims=True)
    scale = lax.rsqrt(spread + EPSILON)
    return centred * scale, scale


def forward_step(x, halos, senders, receivers, weights, bias, gain, hidden_ref, slope_ref):
    rows = x.shape[0]
    slots = senders.shape[1]
    extended = jnp.concatenate([x] + halos, axis=0)
    width = extended.shape[0]
    projected = jnp.concatenate(
        [halves(matmul(extended, weights[0])), halves(matmul(x, weights[1]))], axis=0
    )
    for first in range(0, slots, CHUNK):
        marks = jnp.concatenate(
            [
                one_hot_rows(senders[:, first : first + CHUNK], width),
                one_hot_rows(receivers[:, first : first + CHUNK], rows),
            ],
            axis=1,
        )
        pre_act = joined(matmul(marks, projected)) + bias
        sigmoid = jax.nn.sigmoid(pre_act)
        hidden_ref[first : first + CHUNK, :] = (pre_act * sigmoid).astype(BF16)
        slope_ref[first : first + CHUNK, :] = sigmoid * (1.0 + pre_act * (1.0 - sigmoid))
    hidden = hidden_ref[...]
    gathered = jnp.concatenate(
        [
            matmul(one_hot_columns(receivers, first, CHUNK), hidden)
            for first in range(0, rows, CHUNK)
        ],
        axis=0,
    )
    edge_sums = halves(gathered)
    agg = matmul(edge_sums, jnp.concatenate([weights[2], weights[2]], axis=0)).astype(BF16)
    both = jnp.concatenate([x, agg], axis=1)
    node_pre = matmul(both, jnp.concatenate([weights[3], weights[4]], axis=0))
    normed, _ = normalise(node_pre)
    output = (x.astype(F32) + gain * normed).astype(BF16)
    return output, edge_sums, agg, node_pre


def backward_step(
    upstream,
    x,
    halos,
    senders,
    receivers,
    weights,
    gain,
    edge_sums,
    agg,
    node_pre,
    slope_ref,
    act_ref,
    grads_ref,
    want_input,
):
    rows = x.shape[0]
    slots = senders.shape[1]
    normed, scale = normalise(node_pre)
    grad_gain = jnp.sum(upstream * normed, axis=0, keepdims=True)
    seed = upstream * gain
    grad_pre = scale * (
        seed
        - jnp.mean(seed, axis=1, keepdims=True)
        - normed * jnp.mean(seed * normed, axis=1, keepdims=True)
    )
    pre_parts = halves(grad_pre)
    both = jnp.concatenate([x, agg], axis=1)
    terms = joined(matmul_tn(both, pre_parts))
    grads_ref[3 * H : 5 * H, :] = terms
    back = matmul_nt(pre_parts, jnp.concatenate([twice(weights[4]), twice(weights[3])], axis=0))
    agg_parts = halves(back[:, :H])
    quads = matmul_tn(edge_sums, agg_parts)
    grads_ref[2 * H : 3 * H, :] = joined(quads[:H] + quads[H:])
    message_parts = halves(matmul_nt(agg_parts, twice(weights[2])))
    for first in range(0, slots, CHUNK):
        marks = one_hot_rows(receivers[:, first : first + CHUNK], rows)
        grad_act = joined(matmul(marks, message_parts)) * slope_ref[first : first + CHUNK, :]
        act_ref[first : first + CHUNK, :] = halves(grad_act)
    act = act_ref[...]
    extended = jnp.concatenate([x] + halos, axis=0)
    width = extended.shape[0]
    send_parts = halves(
        jnp.concatenate(
            [
                joined(matmul(one_hot_columns(senders, first, CHUNK), act))
                for first in range(0, width, CHUNK)
            ],
            axis=0,
        )
    )
    grad_recv = jnp.concatenate(
        [
            joined(matmul(one_hot_columns(receivers, first, CHUNK), act))
            for first in range(0, rows, CHUNK)
        ],
        axis=0,
    )
    recv_parts = halves(grad_recv)
    grads_ref[0:H, :] = joined(matmul_tn(extended, send_parts))
    grads_ref[H : 2 * H, :] = joined(matmul_tn(x, recv_parts))
    grad_bias = jnp.sum(grad_recv, axis=0, keepdims=True)
    grads_ref[5 * H :, :] = jnp.concatenate(
        [grad_bias, grad_gain, jnp.zeros((GRAD_ROWS - 5 * H - 2, H), F32)], axis=0
    )
    if not want_input:
        return None, None
    grad_ext = matmul_nt(send_parts, twice(weights[0]))
    grad_nodes = (
        upstream + back[:, H:] + matmul_nt(recv_parts, twice(weights[1])) + grad_ext[:rows]
    )
    return grad_nodes, grad_ext[rows:]


def pool_counts(pool_row):
    shape = (NC_DEV, pool_row.shape[1])
    marks = lax.broadcasted_iota(jnp.int32, shape, 0) == jnp.broadcast_to(pool_row, shape)
    return jnp.sum(jnp.where(marks, 1.0, 0.0), axis=1, keepdims=True)


def send_blocks(source_ref, blocks_ref, out_refs):
    for direction, out_ref in enumerate(out_refs):
        start = pl.multiple_of(blocks_ref[direction] * BLOCK, BLOCK)
        out_ref[...] = source_ref[pl.ds(start, BLOCK), :]


def live_receivers(edges_ref, live_ref):
    receivers = edges_ref[1:2, :]
    slot = lax.broadcasted_iota(jnp.int32, receivers.shape, 1)
    return jnp.where(slot < live_ref[0], receivers, -1)


def fine_ahead(
    live_ref, blocks_ref, x_ref, h0, h1, h2, h3, edges_ref, pool_ref, w_ref, bias_ref, gain_ref,
    mid_ref, coarse_ref, s0, s1, s2, s3, sums_ref, agg_ref, pre_ref, slope_ref,
    hidden_ref,
):
    output, edge_sums, agg, node_pre = forward_step(
        x_ref[...],
        [h0[...], h1[...], h2[...], h3[...]],
        edges_ref[0:1, :],
        live_receivers(edges_ref, live_ref),
        w_ref,
        bias_ref[...],
        gain_ref[...],
        hidden_ref,
        slope_ref,
    )
    mid_ref[...] = output
    sums_ref[...] = edge_sums
    agg_ref[...] = agg
    pre_ref[...] = node_pre
    pool_row = pool_ref[...]
    pooled = matmul(one_hot_columns(pool_row, 0, NC_DEV), output)
    coarse_ref[...] = (pooled / pool_counts(pool_row)).astype(BF16)
    send_blocks(coarse_ref, blocks_ref, (s0, s1, s2, s3))


def coarse_ahead(
    blocks_ref, x_ref, h0, h1, h2, h3, edges_ref, w_ref, bias_ref, gain_ref,
    out_ref, s0, s1, s2, s3, sums_ref, agg_ref, pre_ref, slope_ref,
    hidden_ref,
):
    output, edge_sums, agg, node_pre = forward_step(
        x_ref[...],
        [h0[...], h1[...], h2[...], h3[...]],
        edges_ref[0:1, :],
        edges_ref[1:2, :],
        w_ref.at[0],
        bias_ref[0:1, :],
        gain_ref[0:1, :],
        hidden_ref,
        slope_ref,
    )
    out_ref[...] = output
    sums_ref[...] = edge_sums
    agg_ref[...] = agg
    pre_ref[...] = node_pre
    send_blocks(out_ref, blocks_ref, (s0, s1, s2, s3))


def put_halo_grads(grad_halo, out_refs):
    for group, out_ref in enumerate(out_refs):
        out_ref[...] = grad_halo[group * BLOCK : (group + 1) * BLOCK].astype(BF16)


def coarse_turn(
    loss_scale, x_ref, h0, h1, h2, h3, edges_ref, w_ref, bias_ref, gain_ref, pool_ref, mid_ref, cot_ref,
    out_ref, grad_ref, g0, g1, g2, g3, grads_ref,
    hidden_ref, slope_ref, act_ref,
):
    x = x_ref[...]
    halos = [h0[...], h1[...], h2[...], h3[...]]
    senders, receivers = edges_ref[0:1, :], edges_ref[1:2, :]
    gain = gain_ref[1:2, :]
    weights = w_ref.at[1]
    output, edge_sums, agg, node_pre = forward_step(
        x, halos, senders, receivers, weights, bias_ref[1:2, :], gain, hidden_ref, slope_ref
    )
    pool_row = pool_ref[...]
    lifted = matmul(one_hot_rows(pool_row, NC_DEV), output)
    out_ref[...] = (mid_ref[...].astype(F32) + lifted).astype(BF16)
    upstream = matmul(one_hot_columns(pool_row, 0, NC_DEV), cot_ref[...]) * loss_scale
    grad_nodes, grad_halo = backward_step(
        upstream, x, halos, senders, receivers, weights, gain, edge_sums, agg, node_pre,
        slope_ref, act_ref, grads_ref, True,
    )
    grad_ref[...] = grad_nodes
    put_halo_grads(grad_halo, (g0, g1, g2, g3))


def add_returned(grad_ref, returned, blocks_ref, total_ref):
    total_ref[...] = grad_ref[...]
    for direction, piece in enumerate(returned):
        start = pl.multiple_of(blocks_ref[direction] * BLOCK, BLOCK)
        total_ref[pl.ds(start, BLOCK), :] += piece[...].astype(F32)


def coarse_behind(
    blocks_ref, grad_in_ref, r0, r1, r2, r3, x_ref, h0, h1, h2, h3, edges_ref, w_ref, gain_ref,
    sums_ref, agg_ref, pre_ref, slope_ref,
    grad_ref, g0, g1, g2, g3, grads_ref,
    total_ref, act_ref,
):
    add_returned(grad_in_ref, (r0, r1, r2, r3), blocks_ref, total_ref)
    grad_nodes, grad_halo = backward_step(
        total_ref[...],
        x_ref[...],
        [h0[...], h1[...], h2[...], h3[...]],
        edges_ref[0:1, :],
        edges_ref[1:2, :],
        w_ref.at[0],
        gain_ref[0:1, :],
        sums_ref[...],
        agg_ref[...],
        pre_ref[...],
        slope_ref,
        act_ref,
        grads_ref,
        True,
    )
    grad_ref[...] = grad_nodes
    put_halo_grads(grad_halo, (g0, g1, g2, g3))


def fine_behind(
    loss_scale, root, live_ref, blocks_ref, grad_in_ref, r0, r1, r2, r3, x_ref, h0, h1, h2, h3, edges_ref,
    pool_ref, cot_ref, w_ref, gain_ref, sums_ref, agg_ref, pre_ref, slope_ref,
    pooled_ref, grads_ref,
    total_ref, act_ref,
):
    add_returned(grad_in_ref, (r0, r1, r2, r3), blocks_ref, total_ref)
    total = total_ref[...]
    pooled_ref[...] = total * root
    pool_row = pool_ref[...]
    shared = halves(total / pool_counts(pool_row))
    upstream = cot_ref[...].astype(F32) * loss_scale + joined(
        matmul(one_hot_rows(pool_row, NC_DEV), shared)
    )
    backward_step(
        upstream,
        x_ref[...],
        [h0[...], h1[...], h2[...], h3[...]],
        edges_ref[0:1, :],
        live_receivers(edges_ref, live_ref),
        w_ref,
        gain_ref[...],
        sums_ref[...],
        agg_ref[...],
        pre_ref[...],
        slope_ref,
        act_ref,
        grads_ref,
        False,
    )


def call(kernel, scalars, arrays, outs, scratch):
    vmem = pl.BlockSpec(memory_space=pltpu.VMEM)
    smem = pl.BlockSpec(memory_space=pltpu.SMEM)
    return pl.pallas_call(
        kernel,
        out_shape=[jax.ShapeDtypeStruct(shape, dtype) for shape, dtype in outs],
        in_specs=[smem] * len(scalars) + [vmem] * len(arrays),
        out_specs=[vmem] * len(outs),
        scratch_shapes=[pltpu.VMEM(shape, dtype) for shape, dtype in scratch],
        compiler_params=pltpu.CompilerParams(vmem_limit_bytes=40 * 1024 * 1024),
    )(*scalars, *arrays)


def exchange(pieces):
    received = []
    for axis, (lower, upper) in (("gx", pieces[0:2]), ("gy", pieces[2:4])):
        peers = lax.axis_size(axis)
        up = [(i, i + 1) for i in range(peers - 1)]
        down = [(i + 1, i) for i in range(peers - 1)]
        received.append(lax.ppermute(upper, axis, up))
        received.append(lax.ppermute(lower, axis, down))
    return received


def reduce_all(terms):
    return lax.psum(terms, ("gx", "gy"))


def body(
    fine_nodes,
    fine_edges,
    fine_live,
    fine_halo,
    pool_map,
    coarse_edges,
    coarse_halo,
    fine_weights,
    fine_bias,
    fine_gain,
    coarse_weights,
    coarse_bias,
    coarse_gain,
    cotangent,
):
    x = fine_nodes[0, 0]
    edges = fine_edges[0, 0]
    live = fine_live.reshape(1)
    pool = pool_map[0]
    coarse_list = coarse_edges[0, 0]
    blocks = coarse_halo.reshape(4)
    cot = cotangent[0, 0]
    bias = fine_bias.reshape(1, H)
    gain = fine_gain.reshape(1, H)
    rows, slots, coarse_slots = x.shape[0], edges.shape[1], coarse_list.shape[1]
    total_nodes = rows * lax.axis_size("gx") * lax.axis_size("gy")
    root = math.sqrt(total_nodes)
    block = ((BLOCK, H), BF16)

    def saved(count, edge_count):
        return [
            ((count, 2 * H), BF16),
            ((count, H), BF16),
            ((count, H), F32),
            ((edge_count, H), F32),
        ]

    picks = fine_halo.reshape(4)
    sends = [
        lax.dynamic_slice_in_dim(x, picks[direction] * BLOCK, BLOCK) for direction in range(4)
    ]
    halos = exchange(sends)
    fine_out = call(
        fine_ahead,
        [live, blocks],
        [x, *halos, edges, pool, fine_weights, bias, gain],
        [((rows, H), BF16), ((NC_DEV, H), BF16)] + [block] * 4 + saved(rows, slots),
        [((slots, H), BF16)],
    )
    mid, coarse_0, sends, fine_saved = fine_out[0], fine_out[1], fine_out[2:6], fine_out[6:]
    halos_0 = exchange(sends)
    ahead = call(
        coarse_ahead,
        [blocks],
        [coarse_0, *halos_0, coarse_list, coarse_weights, coarse_bias, coarse_gain],
        [((NC_DEV, H), BF16)] + [block] * 4 + saved(NC_DEV, coarse_slots),
        [((coarse_slots, H), BF16)],
    )
    coarse_1, sends, coarse_saved = ahead[0], ahead[1:5], ahead[5:]
    halos_1 = exchange(sends)
    grads = ((GRAD_ROWS, H), F32)
    turned = call(
        functools.partial(coarse_turn, 1.0 / root),
        [],
        [coarse_1, *halos_1, coarse_list, coarse_weights, coarse_bias, coarse_gain, pool, mid, cot],
        [((rows, H), BF16), ((NC_DEV, H), F32)] + [block] * 4 + [grads],
        [((coarse_slots, H), BF16), ((coarse_slots, H), F32), ((coarse_slots, 2 * H), BF16)],
    )
    result, grad_nodes, grad_halo, grads_1 = turned[0], turned[1], turned[2:6], turned[6]
    returned = exchange(grad_halo)
    behind = call(
        coarse_behind,
        [blocks],
        [grad_nodes, *returned, coarse_0, *halos_0, coarse_list]
        + [coarse_weights, coarse_gain, *coarse_saved],
        [((NC_DEV, H), F32)] + [block] * 4 + [grads],
        [((NC_DEV, H), F32), ((coarse_slots, 2 * H), BF16)],
    )
    grad_nodes, grad_halo, grads_0 = behind[0], behind[1:5], behind[5]
    returned = exchange(grad_halo)
    grad_pooled, grads_f = call(
        functools.partial(fine_behind, 1.0 / root, root),
        [live, blocks],
        [grad_nodes, *returned, x, *halos, edges, pool, cot, fine_weights, gain, *fine_saved],
        [((NC_DEV, H), F32), grads],
        [((NC_DEV, H), F32), ((slots, 2 * H), BF16)],
    )
    total = reduce_all(jnp.concatenate([grads_f, grads_0, grads_1], axis=0))
    total = total.reshape(3, GRAD_ROWS, H)
    weights = total[:, : 5 * H].reshape(3, 5, H, H)
    return (
        result[None, None],
        weights[0],
        total[0, 5 * H],
        total[0, 5 * H + 1],
        weights[1:],
        total[1:, 5 * H],
        total[1:, 5 * H + 1],
        grad_pooled[None, None],
    )


def solution(mesh):
    tiled = P("gx", "gy", None, None)
    return jax.shard_map(
        body,
        mesh=mesh,
        in_specs=(
            tiled,
            tiled,
            P("gx", "gy"),
            tiled,
            P("gx", "gy", None),
            tiled,
            tiled,
            P(),
            P(),
            P(),
            P(),
            P(),
            P(),
            tiled,
        ),
        out_specs=(tiled, P(), P(), P(), P(), P(), P(), tiled),
        check_vma=False,
    )
```

```python
import functools
import math

import jax
import jax.numpy as jnp
from jax import lax
from jax.experimental import pallas as pl
from jax.experimental.pallas import tpu as pltpu
from jax.sharding import PartitionSpec as P

BLOCK = 128
H = 128
COARSE_STEPS = 2
NC_DEV = 256
CHUNK = 256
GRAD_ROWS = 5 * H + 8
PACKED = 2048
SMALL = 15 * H
EPSILON = 1e-05
F32 = jnp.float32
BF16 = jnp.bfloat16
GATHER_WIRE = BF16


def halves(values):
    high = values.astype(BF16)
    low = (values - high.astype(F32)).astype(BF16)
    return jnp.concatenate([high, low], axis=1)


def joined(values):
    return values[:, :H] + values[:, H:]


def matmul(left, right):
    return jnp.dot(left, right, preferred_element_type=F32)


def matmul_nt(left, right):
    return lax.dot_general(left, right, (((1,), (1,)), ((), ())), preferred_element_type=F32)


def matmul_tn(left, right):
    return lax.dot_general(left, right, (((0,), (0,)), ((), ())), preferred_element_type=F32)


def twice(weight):
    return jnp.concatenate([weight, weight], axis=1)


def column_of(row):
    pieces = []
    for start in range(0, row.shape[1], 128):
        wide = jnp.broadcast_to(row[:, start : start + 128], (128, 128))
        pieces.append(wide.T)
    return pieces[0] if len(pieces) == 1 else jnp.concatenate(pieces, axis=0)


def one_hot_rows(row, width):
    spread = column_of(row)
    spread = spread - lax.broadcasted_iota(jnp.int32, spread.shape, 1)
    tiles = [jnp.where(spread == start, 1.0, 0.0).astype(BF16) for start in range(0, width, 128)]
    return jnp.concatenate(tiles, axis=1)


def one_hot_columns(row, first, count):
    shape = (count, row.shape[1])
    marks = lax.broadcasted_iota(jnp.int32, shape, 0) + first == jnp.broadcast_to(row, shape)
    return jnp.where(marks, 1.0, 0.0).astype(BF16)


def place():
    across, along = lax.axis_index("gx") % 2, lax.axis_index("gy") % 2
    return (3 - along, 2 + along, across, 1 - across)


def rows_at(index, count):
    return pl.ds(pl.multiple_of(index * count, count), count)


def gather_halos(x_ref, halos, extended_ref):
    rows = x_ref.shape[0]
    extended_ref[0:rows, :] = x_ref[...]
    for group, halo in zip(place(), halos, strict=True):
        extended_ref[pl.ds(pl.multiple_of(rows + group * BLOCK, BLOCK), BLOCK), :] = halo[...]


def normalise(node_pre):
    centred = node_pre - jnp.mean(node_pre, axis=1, keepdims=True)
    spread = jnp.mean(centred * centred, axis=1, keepdims=True)
    scale = lax.rsqrt(spread + EPSILON)
    return centred * scale, scale


def forward_step(x, extended, senders, receivers, weights, bias, gain, hidden_ref, slope_ref):
    rows = x.shape[0]
    slots = senders.shape[1]
    width = extended.shape[0]
    projected = jnp.concatenate(
        [halves(matmul(extended, weights[0])), halves(matmul(x, weights[1]))], axis=0
    )
    for first in range(0, slots, CHUNK):
        marks = jnp.concatenate(
            [
                one_hot_rows(senders[:, first : first + CHUNK], width),
                one_hot_rows(receivers[:, first : first + CHUNK], rows),
            ],
            axis=1,
        )
        pre_act = joined(matmul(marks, projected)) + bias
        sigmoid = jax.nn.sigmoid(pre_act)
        hidden_ref[first : first + CHUNK, :] = (pre_act * sigmoid).astype(BF16)
        slope_ref[first : first + CHUNK, :] = sigmoid * (1.0 + pre_act * (1.0 - sigmoid))
    hidden = hidden_ref[...]
    gathered = jnp.concatenate(
        [
            matmul(one_hot_columns(receivers, first, CHUNK), hidden)
            for first in range(0, rows, CHUNK)
        ],
        axis=0,
    )
    edge_sums = halves(gathered)
    agg = matmul(edge_sums, jnp.concatenate([weights[2], weights[2]], axis=0)).astype(BF16)
    both = jnp.concatenate([x, agg], axis=1)
    node_pre = matmul(both, jnp.concatenate([weights[3], weights[4]], axis=0))
    normed, _ = normalise(node_pre)
    output = (x.astype(F32) + gain * normed).astype(BF16)
    return output, edge_sums, agg, node_pre


def backward_step(
    upstream,
    x,
    extended,
    senders,
    receivers,
    weights,
    gain,
    edge_sums,
    agg,
    node_pre,
    slope_ref,
    act_ref,
    grads_ref,
    want_input,
):
    rows = x.shape[0]
    slots = senders.shape[1]
    normed, scale = normalise(node_pre)
    grad_gain = jnp.sum(upstream * normed, axis=0, keepdims=True)
    seed = upstream * gain
    grad_pre = scale * (
        seed
        - jnp.mean(seed, axis=1, keepdims=True)
        - normed * jnp.mean(seed * normed, axis=1, keepdims=True)
    )
    pre_parts = halves(grad_pre)
    both = jnp.concatenate([x, agg], axis=1)
    terms = joined(matmul_tn(both, pre_parts))
    grads_ref[3 * H : 5 * H, :] = terms
    back = matmul_nt(pre_parts, jnp.concatenate([twice(weights[4]), twice(weights[3])], axis=0))
    agg_parts = halves(back[:, :H])
    quads = matmul_tn(edge_sums, agg_parts)
    grads_ref[2 * H : 3 * H, :] = joined(quads[:H] + quads[H:])
    message_parts = halves(matmul_nt(agg_parts, twice(weights[2])))
    for first in range(0, slots, CHUNK):
        marks = one_hot_rows(receivers[:, first : first + CHUNK], rows)
        grad_act = joined(matmul(marks, message_parts)) * slope_ref[first : first + CHUNK, :]
        act_ref[first : first + CHUNK, :] = halves(grad_act)
    act = act_ref[...]
    width = extended.shape[0]
    send_parts = halves(
        jnp.concatenate(
            [
                joined(matmul(one_hot_columns(senders, first, CHUNK), act))
                for first in range(0, width, CHUNK)
            ],
            axis=0,
        )
    )
    grad_recv = jnp.concatenate(
        [
            joined(matmul(one_hot_columns(receivers, first, CHUNK), act))
            for first in range(0, rows, CHUNK)
        ],
        axis=0,
    )
    recv_parts = halves(grad_recv)
    grads_ref[0:H, :] = joined(matmul_tn(extended, send_parts))
    grads_ref[H : 2 * H, :] = joined(matmul_tn(x, recv_parts))
    grad_bias = jnp.sum(grad_recv, axis=0, keepdims=True)
    grads_ref[5 * H :, :] = jnp.concatenate(
        [grad_bias, grad_gain, jnp.zeros((GRAD_ROWS - 5 * H - 2, H), F32)], axis=0
    )
    if not want_input:
        return None, None
    grad_ext = matmul_nt(send_parts, twice(weights[0]))
    grad_nodes = (
        upstream + back[:, H:] + matmul_nt(recv_parts, twice(weights[1])) + grad_ext[:rows]
    )
    return grad_nodes, grad_ext[rows:]


def pool_counts(pool_row):
    shape = (NC_DEV, pool_row.shape[1])
    marks = lax.broadcasted_iota(jnp.int32, shape, 0) == jnp.broadcast_to(pool_row, shape)
    return jnp.sum(jnp.where(marks, 1.0, 0.0), axis=1, keepdims=True)


def send_blocks(source_ref, blocks_ref, out_refs):
    for direction, out_ref in zip(place(), out_refs, strict=True):
        start = pl.multiple_of(blocks_ref[direction] * BLOCK, BLOCK)
        out_ref[...] = source_ref[pl.ds(start, BLOCK), :]


def live_receivers(edges_ref, live_ref):
    receivers = edges_ref[1:2, :]
    slot = lax.broadcasted_iota(jnp.int32, receivers.shape, 1)
    return jnp.where(slot < live_ref[0], receivers, -1)


def fine_ahead(
    live_ref, blocks_ref, x_ref, h0, h1, h2, h3, edges_ref, pool_ref, w_ref, bias_ref, gain_ref,
    mid_ref, coarse_ref, s0, s1, s2, s3, sums_ref, agg_ref, pre_ref, slope_ref,
    extended_ref, hidden_ref,
):
    gather_halos(x_ref, (h0, h1, h2, h3), extended_ref)
    output, edge_sums, agg, node_pre = forward_step(
        x_ref[...],
        extended_ref[...],
        edges_ref[0:1, :],
        live_receivers(edges_ref, live_ref),
        w_ref,
        bias_ref[...],
        gain_ref[...],
        hidden_ref,
        slope_ref,
    )
    mid_ref[...] = output
    sums_ref[...] = edge_sums
    agg_ref[...] = agg
    pre_ref[...] = node_pre
    pool_row = pool_ref[...]
    pooled = matmul(one_hot_columns(pool_row, 0, NC_DEV), output)
    coarse_ref[...] = (pooled / pool_counts(pool_row)).astype(BF16)
    send_blocks(coarse_ref, blocks_ref, (s0, s1, s2, s3))


def coarse_ahead(
    blocks_ref, x_ref, h0, h1, h2, h3, edges_ref, w_ref, bias_ref, gain_ref,
    out_ref, s0, s1, s2, s3, sums_ref, agg_ref, pre_ref, slope_ref,
    extended_ref, hidden_ref,
):
    gather_halos(x_ref, (h0, h1, h2, h3), extended_ref)
    output, edge_sums, agg, node_pre = forward_step(
        x_ref[...],
        extended_ref[...],
        edges_ref[0:1, :],
        edges_ref[1:2, :],
        w_ref.at[0],
        bias_ref[0:1, :],
        gain_ref[0:1, :],
        hidden_ref,
        slope_ref,
    )
    out_ref[...] = output
    sums_ref[...] = edge_sums
    agg_ref[...] = agg
    pre_ref[...] = node_pre
    send_blocks(out_ref, blocks_ref, (s0, s1, s2, s3))


def put_halo_grads(grad_halo, halo_ref, out_refs):
    halo_ref[...] = grad_halo.astype(BF16)
    for group, out_ref in zip(place(), out_refs, strict=True):
        out_ref[...] = halo_ref[rows_at(group, BLOCK), :]


def coarse_turn(
    loss_scale, x_ref, h0, h1, h2, h3, edges_ref, w_ref, bias_ref, gain_ref, pool_ref, mid_ref, cot_ref,
    out_ref, grad_ref, g0, g1, g2, g3, grads_ref,
    extended_ref, hidden_ref, slope_ref, act_ref, halo_ref,
):
    gather_halos(x_ref, (h0, h1, h2, h3), extended_ref)
    x = x_ref[...]
    extended = extended_ref[...]
    senders, receivers = edges_ref[0:1, :], edges_ref[1:2, :]
    gain = gain_ref[1:2, :]
    weights = w_ref.at[1]
    output, edge_sums, agg, node_pre = forward_step(
        x, extended, senders, receivers, weights, bias_ref[1:2, :], gain, hidden_ref, slope_ref
    )
    pool_row = pool_ref[...]
    lifted = matmul(one_hot_rows(pool_row, NC_DEV), output)
    out_ref[...] = (mid_ref[...].astype(F32) + lifted).astype(BF16)
    upstream = matmul(one_hot_columns(pool_row, 0, NC_DEV), cot_ref[...]) * loss_scale
    grad_nodes, grad_halo = backward_step(
        upstream, x, extended, senders, receivers, weights, gain, edge_sums, agg, node_pre,
        slope_ref, act_ref, grads_ref, True,
    )
    grad_ref[...] = grad_nodes
    put_halo_grads(grad_halo, halo_ref, (g0, g1, g2, g3))


def add_returned(grad_ref, returned, blocks_ref, total_ref):
    total_ref[...] = grad_ref[...]
    for direction, piece in zip(place(), returned, strict=True):
        start = pl.multiple_of(blocks_ref[direction] * BLOCK, BLOCK)
        total_ref[pl.ds(start, BLOCK), :] += piece[...].astype(F32)


def coarse_behind(
    blocks_ref, grad_in_ref, r0, r1, r2, r3, x_ref, h0, h1, h2, h3, edges_ref, w_ref, gain_ref,
    sums_ref, agg_ref, pre_ref, slope_ref,
    grad_ref, g0, g1, g2, g3, grads_ref,
    extended_ref, total_ref, act_ref, halo_ref,
):
    gather_halos(x_ref, (h0, h1, h2, h3), extended_ref)
    add_returned(grad_in_ref, (r0, r1, r2, r3), blocks_ref, total_ref)
    grad_nodes, grad_halo = backward_step(
        total_ref[...],
        x_ref[...],
        extended_ref[...],
        edges_ref[0:1, :],
        edges_ref[1:2, :],
        w_ref.at[0],
        gain_ref[0:1, :],
        sums_ref[...],
        agg_ref[...],
        pre_ref[...],
        slope_ref,
        act_ref,
        grads_ref,
        True,
    )
    grad_ref[...] = grad_nodes
    put_halo_grads(grad_halo, halo_ref, (g0, g1, g2, g3))


def fine_behind(
    loss_scale, root, live_ref, blocks_ref, grad_in_ref, r0, r1, r2, r3, x_ref, h0, h1, h2, h3, edges_ref,
    pool_ref, cot_ref, w_ref, gain_ref, sums_ref, agg_ref, pre_ref, slope_ref, grads_0_ref, grads_1_ref,
    pooled_ref, packed_ref,
    extended_ref, total_ref, act_ref, grads_ref,
):
    gather_halos(x_ref, (h0, h1, h2, h3), extended_ref)
    add_returned(grad_in_ref, (r0, r1, r2, r3), blocks_ref, total_ref)
    total = total_ref[...]
    pooled_ref[...] = total * root
    pool_row = pool_ref[...]
    shared = halves(total / pool_counts(pool_row))
    upstream = cot_ref[...].astype(F32) * loss_scale + joined(
        matmul(one_hot_rows(pool_row, NC_DEV), shared)
    )
    backward_step(
        upstream,
        x_ref[...],
        extended_ref[...],
        edges_ref[0:1, :],
        live_receivers(edges_ref, live_ref),
        w_ref,
        gain_ref[...],
        sums_ref[...],
        agg_ref[...],
        pre_ref[...],
        slope_ref,
        act_ref,
        grads_ref,
        False,
    )
    for index, source in enumerate((grads_ref, grads_0_ref, grads_1_ref)):
        packed_ref[index * 5 * H : (index + 1) * 5 * H, :] = source[0 : 5 * H, :]
        packed_ref[SMALL + index * 8 : SMALL + index * 8 + 8, :] = source[5 * H :, :]
    packed_ref[SMALL + 24 :, :] = jnp.zeros((PACKED - SMALL - 24, H), F32)


def sum_parts(parts_ref, out_ref):
    values = [parts_ref[index] for index in range(parts_ref.shape[0])]
    while len(values) > 1:
        values = [a + b for a, b in zip(values[0::2], values[1::2], strict=True)]
    out_ref[...] = values[0]


def sum_and_spread(parts_ref, out_ref):
    values = [parts_ref[index] for index in range(parts_ref.shape[0])]
    while len(values) > 1:
        values = [a + b for a, b in zip(values[0::2], values[1::2], strict=True)]
    for index in range(out_ref.shape[0]):
        out_ref[index] = values[0]


def spread(piece_ref, out_ref):
    piece = piece_ref[...].astype(out_ref.dtype)
    for index in range(out_ref.shape[0]):
        out_ref[index] = piece


def finish(all_ref, fine_ref, coarse_ref, fb_ref, fg_ref, cb_ref, cg_ref):
    fine_ref[...] = all_ref[0 : 5 * H, :].astype(F32)
    coarse_ref[...] = all_ref[5 * H : SMALL, :].astype(F32)
    small = all_ref[SMALL : SMALL + 32, :].astype(F32)
    fb_ref[...] = small[0:1]
    fg_ref[...] = small[1:2]
    cb_ref[...] = jnp.concatenate([small[8:9], small[16:17]], axis=0)
    cg_ref[...] = jnp.concatenate([small[9:10], small[17:18]], axis=0)


def reduce_all(packed):
    across, along = lax.axis_size("gx"), lax.axis_size("gy")
    rows = PACKED // across
    part = rows // along
    pieces = lax.all_to_all(packed.reshape(across, rows, H), "gx", 0, 0)
    (mine,) = call(sum_parts, [], [pieces], [((rows, H), F32)], [])
    pieces = lax.all_to_all(mine.reshape(along, part, H), "gy", 0, 0)
    (shared,) = call(sum_and_spread, [], [pieces], [((along, part, H), F32)], [])
    mine = lax.all_to_all(shared, "gy", 0, 0).reshape(rows, H)
    (shared,) = call(spread, [], [mine], [((across, rows, H), GATHER_WIRE)], [])
    everything = lax.all_to_all(shared, "gx", 0, 0).reshape(PACKED, H)
    return call(
        finish,
        [],
        [everything],
        [((5 * H, H), F32), ((10 * H, H), F32)] + [((1, H), F32)] * 2 + [((2, H), F32)] * 2,
        [],
    )


def call(kernel, scalars, arrays, outs, scratch):
    vmem = pl.BlockSpec(memory_space=pltpu.VMEM)
    smem = pl.BlockSpec(memory_space=pltpu.SMEM)
    return pl.pallas_call(
        kernel,
        out_shape=[jax.ShapeDtypeStruct(shape, dtype) for shape, dtype in outs],
        in_specs=[smem] * len(scalars) + [vmem] * len(arrays),
        out_specs=[vmem] * len(outs),
        scratch_shapes=[pltpu.VMEM(shape, dtype) for shape, dtype in scratch],
        compiler_params=pltpu.CompilerParams(vmem_limit_bytes=40 * 1024 * 1024),
    )(*scalars, *arrays)


def exchange(pieces):
    received = []
    for piece, (axis, first) in zip(pieces, (("gy", 0), ("gy", 1), ("gx", 1), ("gx", 0)), strict=True):
        pairs = []
        for i in range(first, lax.axis_size(axis) - 1, 2):
            pairs += [(i, i + 1), (i + 1, i)]
        received.append(lax.ppermute(piece, axis, pairs))
    return received


def pick(blocks_ref, x_ref, s0, s1, s2, s3):
    send_blocks(x_ref, blocks_ref, (s0, s1, s2, s3))


def body(
    fine_nodes,
    fine_edges,
    fine_live,
    fine_halo,
    pool_map,
    coarse_edges,
    coarse_halo,
    fine_weights,
    fine_bias,
    fine_gain,
    coarse_weights,
    coarse_bias,
    coarse_gain,
    cotangent,
):
    x = fine_nodes[0, 0]
    edges = fine_edges[0, 0]
    live = fine_live.reshape(1)
    pool = pool_map[0]
    coarse_list = coarse_edges[0, 0]
    blocks = coarse_halo.reshape(4)
    cot = cotangent[0, 0]
    bias = fine_bias.reshape(1, H)
    gain = fine_gain.reshape(1, H)
    rows, slots, coarse_slots = x.shape[0], edges.shape[1], coarse_list.shape[1]
    total_nodes = rows * lax.axis_size("gx") * lax.axis_size("gy")
    root = math.sqrt(total_nodes)
    block = ((BLOCK, H), BF16)

    def saved(count, edge_count):
        return [
            ((count, 2 * H), BF16),
            ((count, H), BF16),
            ((count, H), F32),
            ((edge_count, H), F32),
        ]

    halos = exchange(call(pick, [fine_halo.reshape(4)], [x], [block] * 4, []))
    fine_out = call(
        fine_ahead,
        [live, blocks],
        [x, *halos, edges, pool, fine_weights, bias, gain],
        [((rows, H), BF16), ((NC_DEV, H), BF16)] + [block] * 4 + saved(rows, slots),
        [((rows + 4 * BLOCK, H), BF16), ((slots, H), BF16)],
    )
    mid, coarse_0, sends, fine_saved = fine_out[0], fine_out[1], fine_out[2:6], fine_out[6:]
    halos_0 = exchange(sends)
    coarse_extended = ((NC_DEV + 4 * BLOCK, H), BF16)
    halo_grads = ((4 * BLOCK, H), BF16)
    ahead = call(
        coarse_ahead,
        [blocks],
        [coarse_0, *halos_0, coarse_list, coarse_weights, coarse_bias, coarse_gain],
        [((NC_DEV, H), BF16)] + [block] * 4 + saved(NC_DEV, coarse_slots),
        [coarse_extended, ((coarse_slots, H), BF16)],
    )
    coarse_1, sends, coarse_saved = ahead[0], ahead[1:5], ahead[5:]
    halos_1 = exchange(sends)
    grads = ((GRAD_ROWS, H), F32)
    turned = call(
        functools.partial(coarse_turn, 1.0 / root),
        [],
        [coarse_1, *halos_1, coarse_list, coarse_weights, coarse_bias, coarse_gain, pool, mid, cot],
        [((rows, H), BF16), ((NC_DEV, H), F32)] + [block] * 4 + [grads],
        [coarse_extended, ((coarse_slots, H), BF16), ((coarse_slots, H), F32)]
        + [((coarse_slots, 2 * H), BF16), halo_grads],
    )
    result, grad_nodes, grad_halo, grads_1 = turned[0], turned[1], turned[2:6], turned[6]
    returned = exchange(grad_halo)
    behind = call(
        coarse_behind,
        [blocks],
        [grad_nodes, *returned, coarse_0, *halos_0, coarse_list]
        + [coarse_weights, coarse_gain, *coarse_saved],
        [((NC_DEV, H), F32)] + [block] * 4 + [grads],
        [coarse_extended, ((NC_DEV, H), F32), ((coarse_slots, 2 * H), BF16), halo_grads],
    )
    grad_nodes, grad_halo, grads_0 = behind[0], behind[1:5], behind[5]
    returned = exchange(grad_halo)
    grad_pooled, packed = call(
        functools.partial(fine_behind, 1.0 / root, root),
        [live, blocks],
        [grad_nodes, *returned, x, *halos, edges, pool, cot, fine_weights, gain, *fine_saved]
        + [grads_0, grads_1],
        [((NC_DEV, H), F32), ((PACKED, H), F32)],
        [((rows + 4 * BLOCK, H), BF16), ((NC_DEV, H), F32), ((slots, 2 * H), BF16), grads],
    )
    fine_w, coarse_w, fine_b, fine_g, coarse_b, coarse_g = reduce_all(packed)
    return (
        result[None, None],
        fine_w.reshape(5, H, H),
        fine_b.reshape(H),
        fine_g.reshape(H),
        coarse_w.reshape(2, 5, H, H),
        coarse_b,
        coarse_g,
        grad_pooled[None, None],
    )


def solution(mesh):
    tiled = P("gx", "gy", None, None)
    return jax.shard_map(
        body,
        mesh=mesh,
        in_specs=(
            tiled,
            tiled,
            P("gx", "gy"),
            tiled,
            P("gx", "gy", None),
            tiled,
            tiled,
            P(),
            P(),
            P(),
            P(),
            P(),
            P(),
            tiled,
        ),
        out_specs=(tiled, P(), P(), P(), P(), P(), P(), tiled),
        check_vma=False,
    )
```

```python
import functools
import math

import jax
import jax.numpy as jnp
from jax import lax
from jax.experimental import pallas as pl
from jax.experimental.pallas import tpu as pltpu
from jax.sharding import PartitionSpec as P

BLOCK = 128
H = 128
COARSE_STEPS = 2
NC_DEV = 256
CHUNK = 256
GRAD_ROWS = 5 * H + 8
PACKED = 2048
SMALL = 15 * H
EPSILON = 1e-05
F32 = jnp.float32
BF16 = jnp.bfloat16
GATHER_WIRE = BF16
SCATTER_WIRE = BF16
SCOPED = 24 * 1024 * 1024


def halves(values):
    high = values.astype(BF16)
    low = (values - high.astype(F32)).astype(BF16)
    return jnp.concatenate([high, low], axis=1)


def joined(values):
    return values[:, :H] + values[:, H:]


def matmul(left, right):
    return jnp.dot(left, right, preferred_element_type=F32)


def matmul_nt(left, right):
    return lax.dot_general(left, right, (((1,), (1,)), ((), ())), preferred_element_type=F32)


def matmul_tn(left, right):
    return lax.dot_general(left, right, (((0,), (0,)), ((), ())), preferred_element_type=F32)


def twice(weight):
    return jnp.concatenate([weight, weight], axis=1)


def column_of(row):
    pieces = []
    for start in range(0, row.shape[1], 128):
        wide = jnp.broadcast_to(row[:, start : start + 128], (128, 128))
        pieces.append(wide.T)
    return pieces[0] if len(pieces) == 1 else jnp.concatenate(pieces, axis=0)


def one_hot_rows(row, width):
    spread = column_of(row)
    spread = spread - lax.broadcasted_iota(jnp.int32, spread.shape, 1)
    tiles = [jnp.where(spread == start, 1.0, 0.0).astype(BF16) for start in range(0, width, 128)]
    return jnp.concatenate(tiles, axis=1)


def one_hot_columns(row, first, count):
    shape = (count, row.shape[1])
    marks = lax.broadcasted_iota(jnp.int32, shape, 0) + first == jnp.broadcast_to(row, shape)
    return jnp.where(marks, 1.0, 0.0).astype(BF16)


def place():
    across, along = lax.axis_index("gx") % 2, lax.axis_index("gy") % 2
    return (3 - along, 2 + along, across, 1 - across)


def rows_at(index, count):
    return pl.ds(pl.multiple_of(index * count, count), count)


def gather_halos(x_ref, halos, extended_ref):
    rows = x_ref.shape[0]
    extended_ref[0:rows, :] = x_ref[...]
    for group, halo in zip(place(), halos, strict=True):
        extended_ref[pl.ds(pl.multiple_of(rows + group * BLOCK, BLOCK), BLOCK), :] = halo[...]


def normalise(node_pre):
    centred = node_pre - jnp.mean(node_pre, axis=1, keepdims=True)
    spread = jnp.mean(centred * centred, axis=1, keepdims=True)
    scale = lax.rsqrt(spread + EPSILON)
    return centred * scale, scale


def forward_step(x, extended, senders, receivers, weights, bias, gain, hidden_ref, slope_ref):
    rows = x.shape[0]
    slots = senders.shape[1]
    width = extended.shape[0]
    projected = jnp.concatenate(
        [halves(matmul(extended, weights[0])), halves(matmul(x, weights[1]))], axis=0
    )
    for first in range(0, slots, CHUNK):
        marks = jnp.concatenate(
            [
                one_hot_rows(senders[:, first : first + CHUNK], width),
                one_hot_rows(receivers[:, first : first + CHUNK], rows),
            ],
            axis=1,
        )
        pre_act = joined(matmul(marks, projected)) + bias
        sigmoid = jax.nn.sigmoid(pre_act)
        hidden_ref[first : first + CHUNK, :] = (pre_act * sigmoid).astype(BF16)
        slope_ref[first : first + CHUNK, :] = sigmoid * (1.0 + pre_act * (1.0 - sigmoid))
    hidden = hidden_ref[...]
    gathered = jnp.concatenate(
        [
            matmul(one_hot_columns(receivers, first, CHUNK), hidden)
            for first in range(0, rows, CHUNK)
        ],
        axis=0,
    )
    edge_sums = halves(gathered)
    agg = matmul(edge_sums, jnp.concatenate([weights[2], weights[2]], axis=0)).astype(BF16)
    both = jnp.concatenate([x, agg], axis=1)
    node_pre = matmul(both, jnp.concatenate([weights[3], weights[4]], axis=0))
    normed, _ = normalise(node_pre)
    output = (x.astype(F32) + gain * normed).astype(BF16)
    return output, edge_sums, agg, node_pre


def backward_step(
    upstream,
    x,
    extended,
    senders,
    receivers,
    weights,
    gain,
    edge_sums,
    agg,
    node_pre,
    slope_ref,
    act_ref,
    grads_ref,
    want_input,
):
    rows = x.shape[0]
    slots = senders.shape[1]
    normed, scale = normalise(node_pre)
    grad_gain = jnp.sum(upstream * normed, axis=0, keepdims=True)
    seed = upstream * gain
    grad_pre = scale * (
        seed
        - jnp.mean(seed, axis=1, keepdims=True)
        - normed * jnp.mean(seed * normed, axis=1, keepdims=True)
    )
    pre_parts = halves(grad_pre)
    both = jnp.concatenate([x, agg], axis=1)
    terms = joined(matmul_tn(both, pre_parts))
    grads_ref[3 * H : 5 * H, :] = terms
    back = matmul_nt(pre_parts, jnp.concatenate([twice(weights[4]), twice(weights[3])], axis=0))
    agg_parts = halves(back[:, :H])
    quads = matmul_tn(edge_sums, agg_parts)
    grads_ref[2 * H : 3 * H, :] = joined(quads[:H] + quads[H:])
    message_parts = halves(matmul_nt(agg_parts, twice(weights[2])))
    for first in range(0, slots, CHUNK):
        marks = one_hot_rows(receivers[:, first : first + CHUNK], rows)
        grad_act = joined(matmul(marks, message_parts)) * slope_ref[first : first + CHUNK, :]
        act_ref[first : first + CHUNK, :] = halves(grad_act)
    act = act_ref[...]
    width = extended.shape[0]
    send_parts = halves(
        jnp.concatenate(
            [
                joined(matmul(one_hot_columns(senders, first, CHUNK), act))
                for first in range(0, width, CHUNK)
            ],
            axis=0,
        )
    )
    grad_recv = jnp.concatenate(
        [
            joined(matmul(one_hot_columns(receivers, first, CHUNK), act))
            for first in range(0, rows, CHUNK)
        ],
        axis=0,
    )
    recv_parts = halves(grad_recv)
    grads_ref[0:H, :] = joined(matmul_tn(extended, send_parts))
    grads_ref[H : 2 * H, :] = joined(matmul_tn(x, recv_parts))
    grad_bias = jnp.sum(grad_recv, axis=0, keepdims=True)
    grads_ref[5 * H :, :] = jnp.concatenate(
        [grad_bias, grad_gain, jnp.zeros((GRAD_ROWS - 5 * H - 2, H), F32)], axis=0
    )
    if not want_input:
        return None, None
    grad_ext = matmul_nt(send_parts, twice(weights[0]))
    grad_nodes = (
        upstream + back[:, H:] + matmul_nt(recv_parts, twice(weights[1])) + grad_ext[:rows]
    )
    return grad_nodes, grad_ext[rows:]


def pool_counts(pool_row):
    shape = (NC_DEV, pool_row.shape[1])
    marks = lax.broadcasted_iota(jnp.int32, shape, 0) == jnp.broadcast_to(pool_row, shape)
    return jnp.sum(jnp.where(marks, 1.0, 0.0), axis=1, keepdims=True)


def listed(blocks_ref, direction):
    blocks = blocks_ref[...]
    chosen = lax.broadcasted_iota(jnp.int32, blocks.shape, 1) == direction
    return jnp.sum(jnp.where(chosen, blocks, 0), axis=1, keepdims=True)


def send_blocks(values, blocks_ref, out_refs):
    for direction, out_ref in zip(place(), out_refs, strict=True):
        name = jnp.broadcast_to(listed(blocks_ref, direction), (BLOCK, H))
        piece = values[:BLOCK]
        for block in range(1, NC_DEV // BLOCK):
            piece = jnp.where(name == block, values[block * BLOCK : (block + 1) * BLOCK], piece)
        out_ref[...] = piece.astype(BF16)


def live_receivers(edges_ref, live_ref):
    receivers = edges_ref[1:2, :]
    slot = lax.broadcasted_iota(jnp.int32, receivers.shape, 1)
    return jnp.where(slot < live_ref[0], receivers, -1)


def fine_ahead(
    live_ref, blocks_ref, x_ref, h0, h1, h2, h3, edges_ref, pool_ref, w_ref, bias_ref, gain_ref,
    mid_ref, coarse_ref, s0, s1, s2, s3, sums_ref, agg_ref, pre_ref, slope_ref,
    extended_ref, hidden_ref,
):
    gather_halos(x_ref, (h0, h1, h2, h3), extended_ref)
    output, edge_sums, agg, node_pre = forward_step(
        x_ref[...],
        extended_ref[...],
        edges_ref[0:1, :],
        live_receivers(edges_ref, live_ref),
        w_ref,
        bias_ref[...],
        gain_ref[...],
        hidden_ref,
        slope_ref,
    )
    mid_ref[...] = output
    sums_ref[...] = edge_sums
    agg_ref[...] = agg
    pre_ref[...] = node_pre
    pool_row = pool_ref[...]
    pooled = matmul(one_hot_columns(pool_row, 0, NC_DEV), output)
    coarse = pooled / pool_counts(pool_row)
    coarse_ref[...] = coarse.astype(BF16)
    send_blocks(coarse, blocks_ref, (s0, s1, s2, s3))


def coarse_ahead(
    blocks_ref, x_ref, h0, h1, h2, h3, edges_ref, w_ref, bias_ref, gain_ref,
    out_ref, s0, s1, s2, s3, sums_ref, agg_ref, pre_ref, slope_ref,
    extended_ref, hidden_ref,
):
    gather_halos(x_ref, (h0, h1, h2, h3), extended_ref)
    output, edge_sums, agg, node_pre = forward_step(
        x_ref[...],
        extended_ref[...],
        edges_ref[0:1, :],
        edges_ref[1:2, :],
        w_ref.at[0],
        bias_ref[0:1, :],
        gain_ref[0:1, :],
        hidden_ref,
        slope_ref,
    )
    out_ref[...] = output
    sums_ref[...] = edge_sums
    agg_ref[...] = agg
    pre_ref[...] = node_pre
    send_blocks(output.astype(F32), blocks_ref, (s0, s1, s2, s3))


def put_halo_grads(grad_halo, halo_ref, out_refs):
    halo_ref[...] = grad_halo.astype(BF16)
    for group, out_ref in zip(place(), out_refs, strict=True):
        out_ref[...] = halo_ref[rows_at(group, BLOCK), :]


def coarse_turn(
    loss_scale, x_ref, h0, h1, h2, h3, edges_ref, w_ref, bias_ref, gain_ref, pool_ref, mid_ref, cot_ref,
    out_ref, grad_ref, g0, g1, g2, g3, grads_ref,
    extended_ref, hidden_ref, slope_ref, act_ref, halo_ref,
):
    gather_halos(x_ref, (h0, h1, h2, h3), extended_ref)
    x = x_ref[...]
    extended = extended_ref[...]
    senders, receivers = edges_ref[0:1, :], edges_ref[1:2, :]
    gain = gain_ref[1:2, :]
    weights = w_ref.at[1]
    output, edge_sums, agg, node_pre = forward_step(
        x, extended, senders, receivers, weights, bias_ref[1:2, :], gain, hidden_ref, slope_ref
    )
    pool_row = pool_ref[...]
    lifted = matmul(one_hot_rows(pool_row, NC_DEV), output)
    out_ref[...] = (mid_ref[...].astype(F32) + lifted).astype(BF16)
    upstream = matmul(one_hot_columns(pool_row, 0, NC_DEV), cot_ref[...]) * loss_scale
    grad_nodes, grad_halo = backward_step(
        upstream, x, extended, senders, receivers, weights, gain, edge_sums, agg, node_pre,
        slope_ref, act_ref, grads_ref, True,
    )
    grad_ref[...] = grad_nodes
    put_halo_grads(grad_halo, halo_ref, (g0, g1, g2, g3))


def add_returned(grad_ref, returned, blocks_ref, total_ref):
    total_ref[...] = grad_ref[...]
    for direction, piece in zip(place(), returned, strict=True):
        name = jnp.broadcast_to(listed(blocks_ref, direction), (BLOCK, H))
        values = piece[...].astype(F32)
        for block in range(NC_DEV // BLOCK):
            total_ref[block * BLOCK : (block + 1) * BLOCK, :] += jnp.where(name == block, values, 0.0)


def coarse_behind(
    blocks_ref, grad_in_ref, r0, r1, r2, r3, x_ref, h0, h1, h2, h3, edges_ref, w_ref, gain_ref,
    sums_ref, agg_ref, pre_ref, slope_ref,
    grad_ref, g0, g1, g2, g3, grads_ref,
    extended_ref, total_ref, act_ref, halo_ref,
):
    gather_halos(x_ref, (h0, h1, h2, h3), extended_ref)
    add_returned(grad_in_ref, (r0, r1, r2, r3), blocks_ref, total_ref)
    grad_nodes, grad_halo = backward_step(
        total_ref[...],
        x_ref[...],
        extended_ref[...],
        edges_ref[0:1, :],
        edges_ref[1:2, :],
        w_ref.at[0],
        gain_ref[0:1, :],
        sums_ref[...],
        agg_ref[...],
        pre_ref[...],
        slope_ref,
        act_ref,
        grads_ref,
        True,
    )
    grad_ref[...] = grad_nodes
    put_halo_grads(grad_halo, halo_ref, (g0, g1, g2, g3))


def fine_behind(
    loss_scale, root, live_ref, blocks_ref, grad_in_ref, r0, r1, r2, r3, x_ref, h0, h1, h2, h3, edges_ref,
    pool_ref, cot_ref, w_ref, gain_ref, sums_ref, agg_ref, pre_ref, slope_ref, grads_0_ref, grads_1_ref,
    pooled_ref, packed_ref,
    extended_ref, total_ref, act_ref, grads_ref,
):
    gather_halos(x_ref, (h0, h1, h2, h3), extended_ref)
    add_returned(grad_in_ref, (r0, r1, r2, r3), blocks_ref, total_ref)
    total = total_ref[...]
    pooled_ref[...] = total * root
    pool_row = pool_ref[...]
    shared = halves(total / pool_counts(pool_row))
    upstream = cot_ref[...].astype(F32) * loss_scale + joined(
        matmul(one_hot_rows(pool_row, NC_DEV), shared)
    )
    backward_step(
        upstream,
        x_ref[...],
        extended_ref[...],
        edges_ref[0:1, :],
        live_receivers(edges_ref, live_ref),
        w_ref,
        gain_ref[...],
        sums_ref[...],
        agg_ref[...],
        pre_ref[...],
        slope_ref,
        act_ref,
        grads_ref,
        False,
    )
    sources = (grads_ref, grads_0_ref, grads_1_ref)
    for index, source in enumerate(sources):
        packed_ref[index * 5 * H : (index + 1) * 5 * H, :] = source[0 : 5 * H, :].astype(SCATTER_WIRE)
    small = [source[5 * H :, :] for source in sources]
    small.append(jnp.zeros((PACKED - SMALL - 24, H), F32))
    packed_ref[SMALL:, :] = jnp.concatenate(small, axis=0).astype(SCATTER_WIRE)


def sum_parts(parts_ref, out_ref):
    values = [parts_ref[index].astype(F32) for index in range(parts_ref.shape[0])]
    while len(values) > 1:
        values = [a + b for a, b in zip(values[0::2], values[1::2], strict=True)]
    out_ref[...] = values[0]


def sum_and_spread(parts_ref, out_ref):
    values = [parts_ref[index].astype(F32) for index in range(parts_ref.shape[0])]
    while len(values) > 1:
        values = [a + b for a, b in zip(values[0::2], values[1::2], strict=True)]
    for index in range(out_ref.shape[0]):
        out_ref[index] = values[0]


def spread(piece_ref, out_ref):
    piece = piece_ref[...].astype(out_ref.dtype)
    for index in range(out_ref.shape[0]):
        out_ref[index] = piece


def finish(all_ref, fine_ref, coarse_ref, fb_ref, fg_ref, cb_ref, cg_ref):
    fine_ref[...] = all_ref[0 : 5 * H, :].astype(F32)
    coarse_ref[...] = all_ref[5 * H : SMALL, :].astype(F32)
    small = all_ref[SMALL : SMALL + 32, :].astype(F32)
    fb_ref[...] = small[0:1]
    fg_ref[...] = small[1:2]
    cb_ref[...] = jnp.concatenate([small[8:9], small[16:17]], axis=0)
    cg_ref[...] = jnp.concatenate([small[9:10], small[17:18]], axis=0)


def reduce_all(packed):
    across, along = lax.axis_size("gx"), lax.axis_size("gy")
    rows = PACKED // across
    part = rows // along
    pieces = lax.all_to_all(packed.reshape(across, rows, H), "gx", 0, 0)
    (mine,) = call(sum_parts, [], [pieces], [((rows, H), F32)], [])
    pieces = lax.all_to_all(mine.reshape(along, part, H), "gy", 0, 0)
    (shared,) = call(sum_and_spread, [], [pieces], [((along, part, H), F32)], [])
    mine = lax.all_to_all(shared, "gy", 0, 0).reshape(rows, H)
    (shared,) = call(spread, [], [mine], [((across, rows, H), GATHER_WIRE)], [])
    everything = lax.all_to_all(shared, "gx", 0, 0).reshape(PACKED, H)
    return call(
        finish,
        [],
        [everything],
        [((5 * H, H), F32), ((10 * H, H), F32)] + [((1, H), F32)] * 2 + [((2, H), F32)] * 2,
        [],
    )


def call(kernel, scalars, arrays, outs, scratch):
    vmem = pl.BlockSpec(memory_space=pltpu.VMEM)
    smem = pl.BlockSpec(memory_space=pltpu.SMEM)
    return pl.pallas_call(
        kernel,
        out_shape=[jax.ShapeDtypeStruct(shape, dtype) for shape, dtype in outs],
        in_specs=[smem] * len(scalars) + [vmem] * len(arrays),
        out_specs=[vmem] * len(outs),
        scratch_shapes=[pltpu.VMEM(shape, dtype) for shape, dtype in scratch],
        compiler_params=pltpu.CompilerParams(vmem_limit_bytes=SCOPED),
    )(*scalars, *arrays)


def exchange(pieces):
    received = []
    for piece, (axis, first) in zip(pieces, (("gy", 0), ("gy", 1), ("gx", 1), ("gx", 0)), strict=True):
        pairs = []
        for i in range(first, lax.axis_size(axis) - 1, 2):
            pairs += [(i, i + 1), (i + 1, i)]
        received.append(lax.ppermute(piece, axis, pairs))
    return received


def stage(*refs):
    blocks_ref, sources = refs[0], refs[1:-2]
    count = (len(sources) - 4) // 2
    sources, pieces, targets = sources[:count], sources[count : count + 4], sources[count + 4 :]
    picks_ref, semaphores = refs[-2:]
    picking = pltpu.make_async_copy(blocks_ref, picks_ref, semaphores.at[0])
    picking.start()
    copies = [
        pltpu.make_async_copy(source, target, semaphores.at[index])
        for index, (source, target) in enumerate(zip(sources, targets, strict=True), 1)
    ]
    for copy in copies:
        copy.start()
    picking.wait()
    for index, (direction, piece) in enumerate(zip(place(), pieces, strict=True), count + 1):
        copy = pltpu.make_async_copy(
            sources[0].at[rows_at(picks_ref[direction], BLOCK), :], piece, semaphores.at[index]
        )
        copy.start()
        copies.append(copy)
    for copy in copies:
        copy.wait()


def staged(picks, arrays):
    hbm = pl.BlockSpec(memory_space=pltpu.HBM)
    vmem = pl.BlockSpec(memory_space=pltpu.VMEM)
    block = jax.ShapeDtypeStruct((BLOCK, H), BF16)
    outs = pl.pallas_call(
        stage,
        out_shape=[block] * 4 + [jax.ShapeDtypeStruct(a.shape, a.dtype) for a in arrays],
        in_specs=[hbm] * (1 + len(arrays)),
        out_specs=[vmem] * (4 + len(arrays)),
        scratch_shapes=[
            pltpu.SMEM(picks.shape, jnp.int32),
            pltpu.SemaphoreType.DMA((5 + len(arrays),)),
        ],
        compiler_params=pltpu.CompilerParams(vmem_limit_bytes=SCOPED),
    )(*[pltpu.with_memory_space_constraint(a, pltpu.HBM) for a in (picks, *arrays)])
    return outs[:4], outs[4:]


def body(
    fine_nodes,
    fine_edges,
    fine_live,
    fine_halo,
    pool_map,
    coarse_edges,
    coarse_halo,
    fine_weights,
    fine_bias,
    fine_gain,
    coarse_weights,
    coarse_bias,
    coarse_gain,
    cotangent,
):
    x = fine_nodes[0, 0]
    edges = fine_edges[0, 0]
    live = fine_live.reshape(1)
    pool = pool_map[0]
    coarse_list = coarse_edges[0, 0]
    blocks = coarse_halo.reshape(1, 4)
    cot = cotangent[0, 0]
    bias = fine_bias.reshape(1, H)
    gain = fine_gain.reshape(1, H)
    rows, slots, coarse_slots = x.shape[0], edges.shape[1], coarse_list.shape[1]
    total_nodes = rows * lax.axis_size("gx") * lax.axis_size("gy")
    root = math.sqrt(total_nodes)
    block = ((BLOCK, H), BF16)

    def saved(count, edge_count):
        return [
            ((count, 2 * H), BF16),
            ((count, H), BF16),
            ((count, H), F32),
            ((edge_count, H), F32),
        ]

    sends, arrays = staged(
        fine_halo.reshape(4),
        [x, edges, pool, coarse_list, blocks, fine_weights, bias, gain]
        + [coarse_weights, coarse_bias, coarse_gain, cot],
    )
    x, edges, pool, coarse_list, blocks, fine_weights, bias, gain = arrays[:8]
    coarse_weights, coarse_bias, coarse_gain, cot = arrays[8:]
    halos = exchange(sends)
    fine_out = call(
        fine_ahead,
        [live],
        [blocks, x, *halos, edges, pool, fine_weights, bias, gain],
        [((rows, H), BF16), ((NC_DEV, H), BF16)] + [block] * 4 + saved(rows, slots),
        [((rows + 4 * BLOCK, H), BF16), ((slots, H), BF16)],
    )
    mid, coarse_0, sends, fine_saved = fine_out[0], fine_out[1], fine_out[2:6], fine_out[6:]
    halos_0 = exchange(sends)
    coarse_extended = ((NC_DEV + 4 * BLOCK, H), BF16)
    halo_grads = ((4 * BLOCK, H), BF16)
    ahead = call(
        coarse_ahead,
        [],
        [blocks, coarse_0, *halos_0, coarse_list, coarse_weights, coarse_bias, coarse_gain],
        [((NC_DEV, H), BF16)] + [block] * 4 + saved(NC_DEV, coarse_slots),
        [coarse_extended, ((coarse_slots, H), BF16)],
    )
    coarse_1, sends, coarse_saved = ahead[0], ahead[1:5], ahead[5:]
    halos_1 = exchange(sends)
    grads = ((GRAD_ROWS, H), F32)
    turned = call(
        functools.partial(coarse_turn, 1.0 / root),
        [],
        [coarse_1, *halos_1, coarse_list, coarse_weights, coarse_bias, coarse_gain, pool, mid, cot],
        [((rows, H), BF16), ((NC_DEV, H), F32)] + [block] * 4 + [grads],
        [coarse_extended, ((coarse_slots, H), BF16), ((coarse_slots, H), F32)]
        + [((coarse_slots, 2 * H), BF16), halo_grads],
    )
    result, grad_nodes, grad_halo, grads_1 = turned[0], turned[1], turned[2:6], turned[6]
    returned = exchange(grad_halo)
    behind = call(
        coarse_behind,
        [],
        [blocks, grad_nodes, *returned, coarse_0, *halos_0, coarse_list]
        + [coarse_weights, coarse_gain, *coarse_saved],
        [((NC_DEV, H), F32)] + [block] * 4 + [grads],
        [coarse_extended, ((NC_DEV, H), F32), ((coarse_slots, 2 * H), BF16), halo_grads],
    )
    grad_nodes, grad_halo, grads_0 = behind[0], behind[1:5], behind[5]
    returned = exchange(grad_halo)
    grad_pooled, packed = call(
        functools.partial(fine_behind, 1.0 / root, root),
        [live],
        [blocks, grad_nodes, *returned, x, *halos, edges, pool, cot, fine_weights, gain, *fine_saved]
        + [grads_0, grads_1],
        [((NC_DEV, H), F32), ((PACKED, H), SCATTER_WIRE)],
        [((rows + 4 * BLOCK, H), BF16), ((NC_DEV, H), F32), ((slots, 2 * H), BF16), grads],
    )
    fine_w, coarse_w, fine_b, fine_g, coarse_b, coarse_g = reduce_all(packed)
    return (
        result[None, None],
        fine_w.reshape(5, H, H),
        fine_b.reshape(H),
        fine_g.reshape(H),
        coarse_w.reshape(2, 5, H, H),
        coarse_b,
        coarse_g,
        grad_pooled[None, None],
    )


def solution(mesh):
    tiled = P("gx", "gy", None, None)
    return jax.shard_map(
        body,
        mesh=mesh,
        in_specs=(
            tiled,
            tiled,
            P("gx", "gy"),
            tiled,
            P("gx", "gy", None),
            tiled,
            tiled,
            P(),
            P(),
            P(),
            P(),
            P(),
            P(),
            tiled,
        ),
        out_specs=(tiled, P(), P(), P(), P(), P(), P(), tiled),
        check_vma=False,
    )
```

```python
import functools
import math

import jax
import jax.numpy as jnp
from jax import lax
from jax.experimental import pallas as pl
from jax.experimental.pallas import tpu as pltpu
from jax.sharding import PartitionSpec as P

BLOCK = 128
H = 128
COARSE_STEPS = 2
NC_DEV = 256
CHUNK = 256
GRAD_ROWS = 5 * H + 8
PACKED = 2048
SMALL = 15 * H
EPSILON = 1e-05
F32 = jnp.float32
BF16 = jnp.bfloat16
GATHER_WIRE = BF16
SCATTER_WIRE = BF16
SCOPED = 24 * 1024 * 1024


def halves(values):
    high = values.astype(BF16)
    low = (values - high.astype(F32)).astype(BF16)
    return jnp.concatenate([high, low], axis=1)


def joined(values):
    return values[:, :H] + values[:, H:]


def matmul(left, right):
    return jnp.dot(left, right, preferred_element_type=F32)


def matmul_nt(left, right):
    return lax.dot_general(left, right, (((1,), (1,)), ((), ())), preferred_element_type=F32)


def matmul_tn(left, right):
    return lax.dot_general(left, right, (((0,), (0,)), ((), ())), preferred_element_type=F32)


def twice(weight):
    return jnp.concatenate([weight, weight], axis=1)


def column_of(row):
    pieces = []
    for start in range(0, row.shape[1], 128):
        wide = jnp.broadcast_to(row[:, start : start + 128], (128, 128))
        pieces.append(wide.T)
    return pieces[0] if len(pieces) == 1 else jnp.concatenate(pieces, axis=0)


def one_hot_rows(row, width):
    spread = column_of(row)
    spread = spread - lax.broadcasted_iota(jnp.int32, spread.shape, 1)
    spread = spread.astype(jnp.int16)
    one, zero = jnp.ones(spread.shape, BF16), jnp.zeros(spread.shape, BF16)
    tiles = [jnp.where(spread == start, one, zero) for start in range(0, width, 128)]
    return jnp.concatenate(tiles, axis=1)


def one_hot_columns(row, first, count):
    shape = (count, row.shape[1])
    wanted = jnp.broadcast_to(row - first, (128, row.shape[1]))
    spread = (wanted - lax.broadcasted_iota(jnp.int32, wanted.shape, 0)).astype(jnp.int16)
    one, zero = jnp.ones(spread.shape, BF16), jnp.zeros(spread.shape, BF16)
    return jnp.concatenate(
        [jnp.where(spread == start, one, zero) for start in range(0, count, 128)], axis=0
    )


def place():
    across, along = lax.axis_index("gx") % 2, lax.axis_index("gy") % 2
    return (2 + along, across, 3 - along, 1 - across)


def rows_at(index, count):
    return pl.ds(pl.multiple_of(index * count, count), count)


def gather_halos(x_ref, halos, extended_ref):
    rows = x_ref.shape[0]
    extended_ref[0:rows, :] = x_ref[...]
    for group, halo in zip(place(), halos, strict=True):
        extended_ref[pl.ds(pl.multiple_of(rows + group * BLOCK, BLOCK), BLOCK), :] = halo[...]


def normalise(node_pre):
    centred = node_pre - jnp.mean(node_pre, axis=1, keepdims=True)
    spread = jnp.mean(centred * centred, axis=1, keepdims=True)
    scale = lax.rsqrt(spread + EPSILON)
    return centred * scale, scale


def forward_step(x, extended, senders, receivers, weights, bias, gain, hidden_ref, slope_ref):
    rows = x.shape[0]
    slots = senders.shape[1]
    width = extended.shape[0]
    projected = jnp.concatenate(
        [halves(matmul(extended, weights[0])), halves(matmul(x, weights[1]))], axis=0
    )
    for first in range(0, slots, CHUNK):
        marks = jnp.concatenate(
            [
                one_hot_rows(senders[:, first : first + CHUNK], width),
                one_hot_rows(receivers[:, first : first + CHUNK], rows),
            ],
            axis=1,
        )
        pre_act = joined(matmul(marks, projected)) + bias
        sigmoid = jax.nn.sigmoid(pre_act)
        hidden_ref[first : first + CHUNK, :] = (pre_act * sigmoid).astype(BF16)
        slope_ref[first : first + CHUNK, :] = sigmoid * (1.0 + pre_act * (1.0 - sigmoid))
    hidden = hidden_ref[...]
    gathered = jnp.concatenate(
        [
            matmul(one_hot_columns(receivers, first, CHUNK), hidden)
            for first in range(0, rows, CHUNK)
        ],
        axis=0,
    )
    edge_sums = halves(gathered)
    agg = matmul(edge_sums, jnp.concatenate([weights[2], weights[2]], axis=0)).astype(BF16)
    both = jnp.concatenate([x, agg], axis=1)
    node_pre = matmul(both, jnp.concatenate([weights[3], weights[4]], axis=0))
    normed, _ = normalise(node_pre)
    output = (x.astype(F32) + gain * normed).astype(BF16)
    return output, edge_sums, agg, node_pre


def backward_step(
    upstream,
    x,
    extended,
    senders,
    receivers,
    weights,
    gain,
    edge_sums,
    agg,
    node_pre,
    slope_ref,
    act_ref,
    grads_ref,
    want_input,
):
    rows = x.shape[0]
    slots = senders.shape[1]
    normed, scale = normalise(node_pre)
    grad_gain = jnp.sum(upstream * normed, axis=0, keepdims=True)
    seed = upstream * gain
    grad_pre = scale * (
        seed
        - jnp.mean(seed, axis=1, keepdims=True)
        - normed * jnp.mean(seed * normed, axis=1, keepdims=True)
    )
    pre_parts = halves(grad_pre)
    both = jnp.concatenate([x, agg], axis=1)
    terms = joined(matmul_tn(both, pre_parts))
    grads_ref[3 * H : 5 * H, :] = terms
    back = matmul_nt(pre_parts, jnp.concatenate([twice(weights[4]), twice(weights[3])], axis=0))
    agg_parts = halves(back[:, :H])
    quads = matmul_tn(edge_sums, agg_parts)
    grads_ref[2 * H : 3 * H, :] = joined(quads[:H] + quads[H:])
    message_parts = halves(matmul_nt(agg_parts, twice(weights[2])))
    for first in range(0, slots, CHUNK):
        marks = one_hot_rows(receivers[:, first : first + CHUNK], rows)
        grad_act = joined(matmul(marks, message_parts)) * slope_ref[first : first + CHUNK, :]
        act_ref[first : first + CHUNK, :] = halves(grad_act)
    act = act_ref[...]
    width = extended.shape[0]
    send_parts = halves(
        jnp.concatenate(
            [
                joined(matmul(one_hot_columns(senders, first, CHUNK), act))
                for first in range(0, width, CHUNK)
            ],
            axis=0,
        )
    )
    grad_recv = jnp.concatenate(
        [
            joined(matmul(one_hot_columns(receivers, first, CHUNK), act))
            for first in range(0, rows, CHUNK)
        ],
        axis=0,
    )
    recv_parts = halves(grad_recv)
    grads_ref[0:H, :] = joined(matmul_tn(extended, send_parts))
    grads_ref[H : 2 * H, :] = joined(matmul_tn(x, recv_parts))
    grad_bias = jnp.sum(grad_recv, axis=0, keepdims=True)
    grads_ref[5 * H :, :] = jnp.concatenate(
        [grad_bias, grad_gain, jnp.zeros((GRAD_ROWS - 5 * H - 2, H), F32)], axis=0
    )
    if not want_input:
        return None, None
    grad_ext = matmul_nt(send_parts, twice(weights[0]))
    grad_nodes = (
        upstream + back[:, H:] + matmul_nt(recv_parts, twice(weights[1])) + grad_ext[:rows]
    )
    return grad_nodes, grad_ext[rows:]


def pool_counts(pool_row):
    shape = (NC_DEV, pool_row.shape[1])
    marks = lax.broadcasted_iota(jnp.int32, shape, 0) == jnp.broadcast_to(pool_row, shape)
    return jnp.sum(jnp.where(marks, 1.0, 0.0), axis=1, keepdims=True)


def listed(blocks_ref, direction):
    blocks = blocks_ref[...]
    chosen = lax.broadcasted_iota(jnp.int32, blocks.shape, 1) == direction
    return jnp.sum(jnp.where(chosen, blocks, 0), axis=1, keepdims=True)


def send_blocks(values, blocks_ref, out_refs):
    for direction, out_ref in zip(place(), out_refs, strict=True):
        name = jnp.broadcast_to(listed(blocks_ref, direction), (BLOCK, H))
        piece = values[:BLOCK]
        for block in range(1, NC_DEV // BLOCK):
            piece = jnp.where(name == block, values[block * BLOCK : (block + 1) * BLOCK], piece)
        out_ref[...] = piece.astype(BF16)


def live_receivers(edges_ref, live_ref):
    receivers = edges_ref[1:2, :]
    slot = lax.broadcasted_iota(jnp.int32, receivers.shape, 1)
    return jnp.where(slot < live_ref[0], receivers, -1)


def fine_ahead(
    live_ref, blocks_ref, x_ref, h0, h1, h2, h3, edges_ref, pool_ref, w_ref, bias_ref, gain_ref,
    mid_ref, coarse_ref, s0, s1, s2, s3, sums_ref, agg_ref, pre_ref, slope_ref,
    extended_ref, hidden_ref,
):
    gather_halos(x_ref, (h0, h1, h2, h3), extended_ref)
    output, edge_sums, agg, node_pre = forward_step(
        x_ref[...],
        extended_ref[...],
        edges_ref[0:1, :],
        live_receivers(edges_ref, live_ref),
        w_ref,
        bias_ref[...],
        gain_ref[...],
        hidden_ref,
        slope_ref,
    )
    mid_ref[...] = output
    sums_ref[...] = edge_sums
    agg_ref[...] = agg
    pre_ref[...] = node_pre
    pool_row = pool_ref[...]
    pooled = matmul(one_hot_columns(pool_row, 0, NC_DEV), output)
    coarse = pooled / pool_counts(pool_row)
    coarse_ref[...] = coarse.astype(BF16)
    send_blocks(coarse, blocks_ref, (s0, s1, s2, s3))


def coarse_ahead(
    blocks_ref, x_ref, h0, h1, h2, h3, edges_ref, w_ref, bias_ref, gain_ref,
    out_ref, s0, s1, s2, s3, sums_ref, agg_ref, pre_ref, slope_ref,
    extended_ref, hidden_ref,
):
    gather_halos(x_ref, (h0, h1, h2, h3), extended_ref)
    output, edge_sums, agg, node_pre = forward_step(
        x_ref[...],
        extended_ref[...],
        edges_ref[0:1, :],
        edges_ref[1:2, :],
        w_ref.at[0],
        bias_ref[0:1, :],
        gain_ref[0:1, :],
        hidden_ref,
        slope_ref,
    )
    out_ref[...] = output
    sums_ref[...] = edge_sums
    agg_ref[...] = agg
    pre_ref[...] = node_pre
    send_blocks(output.astype(F32), blocks_ref, (s0, s1, s2, s3))


def put_halo_grads(grad_halo, halo_ref, out_refs):
    halo_ref[...] = grad_halo.astype(BF16)
    for group, out_ref in zip(place(), out_refs, strict=True):
        out_ref[...] = halo_ref[rows_at(group, BLOCK), :]


def coarse_turn(
    loss_scale, x_ref, h0, h1, h2, h3, edges_ref, w_ref, bias_ref, gain_ref, pool_ref, mid_ref, cot_ref,
    out_ref, grad_ref, g0, g1, g2, g3, grads_ref,
    extended_ref, hidden_ref, slope_ref, act_ref, halo_ref,
):
    gather_halos(x_ref, (h0, h1, h2, h3), extended_ref)
    x = x_ref[...]
    extended = extended_ref[...]
    senders, receivers = edges_ref[0:1, :], edges_ref[1:2, :]
    gain = gain_ref[1:2, :]
    weights = w_ref.at[1]
    output, edge_sums, agg, node_pre = forward_step(
        x, extended, senders, receivers, weights, bias_ref[1:2, :], gain, hidden_ref, slope_ref
    )
    pool_row = pool_ref[...]
    lifted = matmul(one_hot_rows(pool_row, NC_DEV), output)
    out_ref[...] = (mid_ref[...].astype(F32) + lifted).astype(BF16)
    upstream = matmul(one_hot_columns(pool_row, 0, NC_DEV), cot_ref[...]) * loss_scale
    grad_nodes, grad_halo = backward_step(
        upstream, x, extended, senders, receivers, weights, gain, edge_sums, agg, node_pre,
        slope_ref, act_ref, grads_ref, True,
    )
    grad_ref[...] = grad_nodes
    put_halo_grads(grad_halo, halo_ref, (g0, g1, g2, g3))


def add_returned(grad_ref, returned, blocks_ref, total_ref):
    total_ref[...] = grad_ref[...]
    for direction, piece in zip(place(), returned, strict=True):
        name = jnp.broadcast_to(listed(blocks_ref, direction), (BLOCK, H))
        values = piece[...].astype(F32)
        for block in range(NC_DEV // BLOCK):
            total_ref[block * BLOCK : (block + 1) * BLOCK, :] += jnp.where(name == block, values, 0.0)


def coarse_behind(
    blocks_ref, grad_in_ref, r0, r1, r2, r3, x_ref, h0, h1, h2, h3, edges_ref, w_ref, gain_ref,
    sums_ref, agg_ref, pre_ref, slope_ref,
    grad_ref, g0, g1, g2, g3, grads_ref,
    extended_ref, total_ref, act_ref, halo_ref,
):
    gather_halos(x_ref, (h0, h1, h2, h3), extended_ref)
    add_returned(grad_in_ref, (r0, r1, r2, r3), blocks_ref, total_ref)
    grad_nodes, grad_halo = backward_step(
        total_ref[...],
        x_ref[...],
        extended_ref[...],
        edges_ref[0:1, :],
        edges_ref[1:2, :],
        w_ref.at[0],
        gain_ref[0:1, :],
        sums_ref[...],
        agg_ref[...],
        pre_ref[...],
        slope_ref,
        act_ref,
        grads_ref,
        True,
    )
    grad_ref[...] = grad_nodes
    put_halo_grads(grad_halo, halo_ref, (g0, g1, g2, g3))


def fine_behind(
    loss_scale, root, live_ref, blocks_ref, grad_in_ref, r0, r1, r2, r3, x_ref, h0, h1, h2, h3, edges_ref,
    pool_ref, cot_ref, w_ref, gain_ref, sums_ref, agg_ref, pre_ref, slope_ref, grads_0_ref, grads_1_ref,
    pooled_ref, packed_ref,
    extended_ref, total_ref, act_ref, grads_ref,
):
    gather_halos(x_ref, (h0, h1, h2, h3), extended_ref)
    add_returned(grad_in_ref, (r0, r1, r2, r3), blocks_ref, total_ref)
    total = total_ref[...]
    pooled_ref[...] = total * root
    pool_row = pool_ref[...]
    shared = halves(total / pool_counts(pool_row))
    upstream = cot_ref[...].astype(F32) * loss_scale + joined(
        matmul(one_hot_rows(pool_row, NC_DEV), shared)
    )
    backward_step(
        upstream,
        x_ref[...],
        extended_ref[...],
        edges_ref[0:1, :],
        live_receivers(edges_ref, live_ref),
        w_ref,
        gain_ref[...],
        sums_ref[...],
        agg_ref[...],
        pre_ref[...],
        slope_ref,
        act_ref,
        grads_ref,
        False,
    )
    sources = (grads_ref, grads_0_ref, grads_1_ref)
    for index, source in enumerate(sources):
        packed_ref[index * 5 * H : (index + 1) * 5 * H, :] = source[0 : 5 * H, :].astype(SCATTER_WIRE)
    small = [source[5 * H :, :] for source in sources]
    small.append(jnp.zeros((PACKED - SMALL - 24, H), F32))
    packed_ref[SMALL:, :] = jnp.concatenate(small, axis=0).astype(SCATTER_WIRE)


def sum_parts(parts_ref, out_ref):
    values = [parts_ref[index].astype(F32) for index in range(parts_ref.shape[0])]
    while len(values) > 1:
        values = [a + b for a, b in zip(values[0::2], values[1::2], strict=True)]
    out_ref[...] = values[0]


def sum_and_spread(parts_ref, out_ref):
    values = [parts_ref[index].astype(F32) for index in range(parts_ref.shape[0])]
    while len(values) > 1:
        values = [a + b for a, b in zip(values[0::2], values[1::2], strict=True)]
    for index in range(out_ref.shape[0]):
        out_ref[index] = values[0]


def spread(piece_ref, out_ref):
    piece = piece_ref[...].astype(out_ref.dtype)
    for index in range(out_ref.shape[0]):
        out_ref[index] = piece


def finish(all_ref, fine_ref, coarse_ref, fb_ref, fg_ref, cb_ref, cg_ref):
    fine_ref[...] = all_ref[0 : 5 * H, :].astype(F32)
    coarse_ref[...] = all_ref[5 * H : SMALL, :].astype(F32)
    small = all_ref[SMALL : SMALL + 32, :].astype(F32)
    fb_ref[...] = small[0:1]
    fg_ref[...] = small[1:2]
    cb_ref[...] = jnp.concatenate([small[8:9], small[16:17]], axis=0)
    cg_ref[...] = jnp.concatenate([small[9:10], small[17:18]], axis=0)


def reduce_all(packed):
    across, along = lax.axis_size("gx"), lax.axis_size("gy")
    rows = PACKED // across
    part = rows // along
    pieces = lax.all_to_all(packed.reshape(across, rows, H), "gx", 0, 0)
    (mine,) = call(sum_parts, [], [pieces], [((rows, H), F32)], [])
    pieces = lax.all_to_all(mine.reshape(along, part, H), "gy", 0, 0)
    (shared,) = call(sum_and_spread, [], [pieces], [((along, part, H), F32)], [])
    mine = lax.all_to_all(shared, "gy", 0, 0).reshape(rows, H)
    (shared,) = call(spread, [], [mine], [((across, rows, H), GATHER_WIRE)], [])
    everything = lax.all_to_all(shared, "gx", 0, 0).reshape(PACKED, H)
    return call(
        finish,
        [],
        [everything],
        [((5 * H, H), F32), ((10 * H, H), F32)] + [((1, H), F32)] * 2 + [((2, H), F32)] * 2,
        [],
    )


def call(kernel, scalars, arrays, outs, scratch):
    vmem = pl.BlockSpec(memory_space=pltpu.VMEM)
    smem = pl.BlockSpec(memory_space=pltpu.SMEM)
    return pl.pallas_call(
        kernel,
        out_shape=[jax.ShapeDtypeStruct(shape, dtype) for shape, dtype in outs],
        in_specs=[smem] * len(scalars) + [vmem] * len(arrays),
        out_specs=[vmem] * len(outs),
        scratch_shapes=[pltpu.VMEM(shape, dtype) for shape, dtype in scratch],
        compiler_params=pltpu.CompilerParams(vmem_limit_bytes=SCOPED),
    )(*scalars, *arrays)


def exchange(pieces):
    received = []
    for piece, (axis, first) in zip(pieces, (("gy", 1), ("gx", 1), ("gy", 0), ("gx", 0)), strict=True):
        pairs = []
        for i in range(first, lax.axis_size(axis) - 1, 2):
            pairs += [(i, i + 1), (i + 1, i)]
        received.append(lax.ppermute(piece, axis, pairs))
    return received


def stage(*refs):
    blocks_ref, sources = refs[0], refs[1:-2]
    count = (len(sources) - 4) // 2
    sources, pieces, targets = sources[:count], sources[count : count + 4], sources[count + 4 :]
    picks_ref, semaphores = refs[-2:]
    picking = pltpu.make_async_copy(blocks_ref, picks_ref, semaphores.at[0])
    picking.start()
    copies = [
        pltpu.make_async_copy(source, target, semaphores.at[index])
        for index, (source, target) in enumerate(zip(sources, targets, strict=True), 1)
    ]
    for copy in copies:
        copy.start()
    picking.wait()
    copies[0].wait()
    for direction, piece in zip(place(), pieces, strict=True):
        piece[...] = targets[0][rows_at(picks_ref[direction], BLOCK), :]
    for copy in copies[1:]:
        copy.wait()


def staged(picks, arrays):
    hbm = pl.BlockSpec(memory_space=pltpu.HBM)
    vmem = pl.BlockSpec(memory_space=pltpu.VMEM)
    block = jax.ShapeDtypeStruct((BLOCK, H), BF16)
    outs = pl.pallas_call(
        stage,
        out_shape=[block] * 4 + [jax.ShapeDtypeStruct(a.shape, a.dtype) for a in arrays],
        in_specs=[hbm] * (1 + len(arrays)),
        out_specs=[vmem] * (4 + len(arrays)),
        scratch_shapes=[
            pltpu.SMEM(picks.shape, jnp.int32),
            pltpu.SemaphoreType.DMA((1 + len(arrays),)),
        ],
        compiler_params=pltpu.CompilerParams(vmem_limit_bytes=SCOPED),
    )(*[pltpu.with_memory_space_constraint(a, pltpu.HBM) for a in (picks, *arrays)])
    return outs[:4], outs[4:]


def body(
    fine_nodes,
    fine_edges,
    fine_live,
    fine_halo,
    pool_map,
    coarse_edges,
    coarse_halo,
    fine_weights,
    fine_bias,
    fine_gain,
    coarse_weights,
    coarse_bias,
    coarse_gain,
    cotangent,
):
    x = fine_nodes[0, 0]
    edges = fine_edges[0, 0]
    live = fine_live.reshape(1)
    pool = pool_map[0]
    coarse_list = coarse_edges[0, 0]
    blocks = coarse_halo.reshape(1, 4)
    cot = cotangent[0, 0]
    bias = fine_bias.reshape(1, H)
    gain = fine_gain.reshape(1, H)
    rows, slots, coarse_slots = x.shape[0], edges.shape[1], coarse_list.shape[1]
    total_nodes = rows * lax.axis_size("gx") * lax.axis_size("gy")
    root = math.sqrt(total_nodes)
    block = ((BLOCK, H), BF16)

    def saved(count, edge_count):
        return [
            ((count, 2 * H), BF16),
            ((count, H), BF16),
            ((count, H), F32),
            ((edge_count, H), F32),
        ]

    sends, arrays = staged(
        fine_halo.reshape(4),
        [x, edges, pool, coarse_list, blocks, fine_weights, bias, gain]
        + [coarse_weights, coarse_bias, coarse_gain, cot],
    )
    x, edges, pool, coarse_list, blocks, fine_weights, bias, gain = arrays[:8]
    coarse_weights, coarse_bias, coarse_gain, cot = arrays[8:]
    halos = exchange(sends)
    fine_out = call(
        fine_ahead,
        [live],
        [blocks, x, *halos, edges, pool, fine_weights, bias, gain],
        [((rows, H), BF16), ((NC_DEV, H), BF16)] + [block] * 4 + saved(rows, slots),
        [((rows + 4 * BLOCK, H), BF16), ((slots, H), BF16)],
    )
    mid, coarse_0, sends, fine_saved = fine_out[0], fine_out[1], fine_out[2:6], fine_out[6:]
    halos_0 = exchange(sends)
    coarse_extended = ((NC_DEV + 4 * BLOCK, H), BF16)
    halo_grads = ((4 * BLOCK, H), BF16)
    ahead = call(
        coarse_ahead,
        [],
        [blocks, coarse_0, *halos_0, coarse_list, coarse_weights, coarse_bias, coarse_gain],
        [((NC_DEV, H), BF16)] + [block] * 4 + saved(NC_DEV, coarse_slots),
        [coarse_extended, ((coarse_slots, H), BF16)],
    )
    coarse_1, sends, coarse_saved = ahead[0], ahead[1:5], ahead[5:]
    halos_1 = exchange(sends)
    grads = ((GRAD_ROWS, H), F32)
    turned = call(
        functools.partial(coarse_turn, 1.0 / root),
        [],
        [coarse_1, *halos_1, coarse_list, coarse_weights, coarse_bias, coarse_gain, pool, mid, cot],
        [((rows, H), BF16), ((NC_DEV, H), F32)] + [block] * 4 + [grads],
        [coarse_extended, ((coarse_slots, H), BF16), ((coarse_slots, H), F32)]
        + [((coarse_slots, 2 * H), BF16), halo_grads],
    )
    result, grad_nodes, grad_halo, grads_1 = turned[0], turned[1], turned[2:6], turned[6]
    returned = exchange(grad_halo)
    behind = call(
        coarse_behind,
        [],
        [blocks, grad_nodes, *returned, coarse_0, *halos_0, coarse_list]
        + [coarse_weights, coarse_gain, *coarse_saved],
        [((NC_DEV, H), F32)] + [block] * 4 + [grads],
        [coarse_extended, ((NC_DEV, H), F32), ((coarse_slots, 2 * H), BF16), halo_grads],
    )
    grad_nodes, grad_halo, grads_0 = behind[0], behind[1:5], behind[5]
    returned = exchange(grad_halo)
    grad_pooled, packed = call(
        functools.partial(fine_behind, 1.0 / root, root),
        [live],
        [blocks, grad_nodes, *returned, x, *halos, edges, pool, cot, fine_weights, gain, *fine_saved]
        + [grads_0, grads_1],
        [((NC_DEV, H), F32), ((PACKED, H), SCATTER_WIRE)],
        [((rows + 4 * BLOCK, H), BF16), ((NC_DEV, H), F32), ((slots, 2 * H), BF16), grads],
    )
    fine_w, coarse_w, fine_b, fine_g, coarse_b, coarse_g = reduce_all(packed)
    return (
        result[None, None],
        fine_w.reshape(5, H, H),
        fine_b.reshape(H),
        fine_g.reshape(H),
        coarse_w.reshape(2, 5, H, H),
        coarse_b,
        coarse_g,
        grad_pooled[None, None],
    )


def solution(mesh):
    tiled = P("gx", "gy", None, None)
    return jax.shard_map(
        body,
        mesh=mesh,
        in_specs=(
            tiled,
            tiled,
            P("gx", "gy"),
            tiled,
            P("gx", "gy", None),
            tiled,
            tiled,
            P(),
            P(),
            P(),
            P(),
            P(),
            P(),
            tiled,
        ),
        out_specs=(tiled, P(), P(), P(), P(), P(), P(), tiled),
        check_vma=False,
    )
```

```python
import functools
import math

import jax
import jax.numpy as jnp
from jax import lax
from jax.experimental import pallas as pl
from jax.experimental.pallas import tpu as pltpu
from jax.sharding import PartitionSpec as P

BLOCK = 128
H = 128
COARSE_STEPS = 2
NC_DEV = 256
CHUNK = 256
GRAD_ROWS = 5 * H + 8
PACKED = 2048
SMALL = 15 * H
EPSILON = 1e-05
F32 = jnp.float32
BF16 = jnp.bfloat16
GATHER_WIRE = BF16
SCATTER_WIRE = BF16
SCOPED = 24 * 1024 * 1024
COST = pl.CostEstimate(flops=1 << 29, bytes_accessed=1 << 20, transcendentals=0)


def halves(values):
    high = values.astype(BF16)
    low = (values - high.astype(F32)).astype(BF16)
    return jnp.concatenate([high, low], axis=1)


def joined(values):
    return values[:, :H] + values[:, H:]


def matmul(left, right):
    return jnp.dot(left, right, preferred_element_type=F32)


def matmul_nt(left, right):
    return lax.dot_general(left, right, (((1,), (1,)), ((), ())), preferred_element_type=F32)


def matmul_tn(left, right):
    return lax.dot_general(left, right, (((0,), (0,)), ((), ())), preferred_element_type=F32)


def twice(weight):
    return jnp.concatenate([weight, weight], axis=1)


def column_of(row):
    pieces = []
    for start in range(0, row.shape[1], 128):
        wide = jnp.broadcast_to(row[:, start : start + 128], (128, 128))
        pieces.append(wide.T)
    return pieces[0] if len(pieces) == 1 else jnp.concatenate(pieces, axis=0)


def one_hot_rows(row, width):
    spread = column_of(row)
    spread = spread - lax.broadcasted_iota(jnp.int32, spread.shape, 1)
    spread = spread.astype(jnp.int16)
    one, zero = jnp.ones(spread.shape, BF16), jnp.zeros(spread.shape, BF16)
    tiles = [jnp.where(spread == start, one, zero) for start in range(0, width, 128)]
    return jnp.concatenate(tiles, axis=1)


def one_hot_columns(row, first, count):
    shape = (count, row.shape[1])
    wanted = jnp.broadcast_to(row - first, (128, row.shape[1]))
    spread = (wanted - lax.broadcasted_iota(jnp.int32, wanted.shape, 0)).astype(jnp.int16)
    one, zero = jnp.ones(spread.shape, BF16), jnp.zeros(spread.shape, BF16)
    return jnp.concatenate(
        [jnp.where(spread == start, one, zero) for start in range(0, count, 128)], axis=0
    )


def place():
    across, along = lax.axis_index("gx") % 2, lax.axis_index("gy") % 2
    return (2 + along, across, 3 - along, 1 - across)


def rows_at(index, count):
    return pl.ds(pl.multiple_of(index * count, count), count)


def gather_halos(x_ref, halos, extended_ref):
    rows = x_ref.shape[0]
    extended_ref[0:rows, :] = x_ref[...]
    for group, halo in zip(place(), halos, strict=True):
        extended_ref[pl.ds(pl.multiple_of(rows + group * BLOCK, BLOCK), BLOCK), :] = halo[...]


def normalise(node_pre):
    centred = node_pre - jnp.mean(node_pre, axis=1, keepdims=True)
    spread = jnp.mean(centred * centred, axis=1, keepdims=True)
    scale = lax.rsqrt(spread + EPSILON)
    return centred * scale, scale


def own_part(step, x_ref, edges_ref, w_ref, own_ref):
    weights = w_ref if step is None else w_ref.at[step]
    x = x_ref[...]
    rows = x.shape[0]
    projected = jnp.concatenate(
        [halves(matmul(x, weights[0])), halves(matmul(x, weights[1]))], axis=0
    )
    for first in range(0, own_ref.shape[0], CHUNK):
        ends = [edges_ref[end : end + 1, first : first + CHUNK] for end in range(2)]
        marks = jnp.concatenate([one_hot_rows(end, rows) for end in ends], axis=1)
        own_ref[first : first + CHUNK, :] = joined(matmul(marks, projected))


def forward_step(x, extended, senders, receivers, weights, bias, gain, own_ref, hidden_ref, slope_ref):
    rows = x.shape[0]
    slots = senders.shape[1]
    width = extended.shape[0] - rows
    projected = halves(matmul(extended[rows:], weights[0]))
    for first in range(0, slots, CHUNK):
        marks = one_hot_rows(senders[:, first : first + CHUNK] - rows, width)
        own = own_ref[first : first + CHUNK, :]
        pre_act = joined(matmul(marks, projected)) + own + bias
        sigmoid = jax.nn.sigmoid(pre_act)
        hidden_ref[first : first + CHUNK, :] = (pre_act * sigmoid).astype(BF16)
        slope_ref[first : first + CHUNK, :] = sigmoid * (1.0 + pre_act * (1.0 - sigmoid))
    hidden = hidden_ref[...]
    gathered = jnp.concatenate(
        [
            matmul(one_hot_columns(receivers, first, CHUNK), hidden)
            for first in range(0, rows, CHUNK)
        ],
        axis=0,
    )
    edge_sums = halves(gathered)
    agg = matmul(edge_sums, jnp.concatenate([weights[2], weights[2]], axis=0)).astype(BF16)
    both = jnp.concatenate([x, agg], axis=1)
    node_pre = matmul(both, jnp.concatenate([weights[3], weights[4]], axis=0))
    normed, _ = normalise(node_pre)
    output = (x.astype(F32) + gain * normed).astype(BF16)
    return output, edge_sums, agg, node_pre


def backward_step(
    upstream,
    x,
    extended,
    senders,
    receivers,
    weights,
    gain,
    edge_sums,
    agg,
    node_pre,
    slope_ref,
    act_ref,
    grads_ref,
    want_input,
):
    rows = x.shape[0]
    slots = senders.shape[1]
    normed, scale = normalise(node_pre)
    grad_gain = jnp.sum(upstream * normed, axis=0, keepdims=True)
    seed = upstream * gain
    grad_pre = scale * (
        seed
        - jnp.mean(seed, axis=1, keepdims=True)
        - normed * jnp.mean(seed * normed, axis=1, keepdims=True)
    )
    pre_parts = halves(grad_pre)
    both = jnp.concatenate([x, agg], axis=1)
    terms = joined(matmul_tn(both, pre_parts))
    grads_ref[3 * H : 5 * H, :] = terms
    back = matmul_nt(pre_parts, jnp.concatenate([twice(weights[4]), twice(weights[3])], axis=0))
    agg_parts = halves(back[:, :H])
    quads = matmul_tn(edge_sums, agg_parts)
    grads_ref[2 * H : 3 * H, :] = joined(quads[:H] + quads[H:])
    message_parts = halves(matmul_nt(agg_parts, twice(weights[2])))
    for first in range(0, slots, CHUNK):
        marks = one_hot_rows(receivers[:, first : first + CHUNK], rows)
        grad_act = joined(matmul(marks, message_parts)) * slope_ref[first : first + CHUNK, :]
        act_ref[first : first + CHUNK, :] = halves(grad_act)
    act = act_ref[...]
    width = extended.shape[0]
    send_parts = halves(
        jnp.concatenate(
            [
                joined(matmul(one_hot_columns(senders, first, CHUNK), act))
                for first in range(0, width, CHUNK)
            ],
            axis=0,
        )
    )
    grad_recv = jnp.concatenate(
        [
            joined(matmul(one_hot_columns(receivers, first, CHUNK), act))
            for first in range(0, rows, CHUNK)
        ],
        axis=0,
    )
    recv_parts = halves(grad_recv)
    grads_ref[0:H, :] = joined(matmul_tn(extended, send_parts))
    grads_ref[H : 2 * H, :] = joined(matmul_tn(x, recv_parts))
    grad_bias = jnp.sum(grad_recv, axis=0, keepdims=True)
    grads_ref[5 * H :, :] = jnp.concatenate(
        [grad_bias, grad_gain, jnp.zeros((GRAD_ROWS - 5 * H - 2, H), F32)], axis=0
    )
    if not want_input:
        return None, None
    grad_ext = matmul_nt(send_parts, twice(weights[0]))
    grad_nodes = (
        upstream + back[:, H:] + matmul_nt(recv_parts, twice(weights[1])) + grad_ext[:rows]
    )
    return grad_nodes, grad_ext[rows:]


def pool_counts(pool_row):
    shape = (NC_DEV, pool_row.shape[1])
    marks = lax.broadcasted_iota(jnp.int32, shape, 0) == jnp.broadcast_to(pool_row, shape)
    return jnp.sum(jnp.where(marks, 1.0, 0.0), axis=1, keepdims=True)


def listed(blocks_ref, direction):
    blocks = blocks_ref[...]
    chosen = lax.broadcasted_iota(jnp.int32, blocks.shape, 1) == direction
    return jnp.sum(jnp.where(chosen, blocks, 0), axis=1, keepdims=True)


def send_blocks(values, blocks_ref, out_refs):
    for direction, out_ref in zip(place(), out_refs, strict=True):
        name = jnp.broadcast_to(listed(blocks_ref, direction), (BLOCK, H))
        piece = values[:BLOCK]
        for block in range(1, NC_DEV // BLOCK):
            piece = jnp.where(name == block, values[block * BLOCK : (block + 1) * BLOCK], piece)
        out_ref[...] = piece.astype(BF16)


def live_receivers(edges_ref, live_ref):
    receivers = edges_ref[1:2, :]
    slot = lax.broadcasted_iota(jnp.int32, receivers.shape, 1)
    return jnp.where(slot < live_ref[0], receivers, -1)


def fine_ahead(
    live_ref, blocks_ref, x_ref, h0, h1, h2, h3, edges_ref, pool_ref, w_ref, bias_ref, gain_ref, own_ref,
    mid_ref, coarse_ref, s0, s1, s2, s3, sums_ref, agg_ref, pre_ref, slope_ref,
    extended_ref, hidden_ref,
):
    gather_halos(x_ref, (h0, h1, h2, h3), extended_ref)
    output, edge_sums, agg, node_pre = forward_step(
        x_ref[...],
        extended_ref[...],
        edges_ref[0:1, :],
        live_receivers(edges_ref, live_ref),
        w_ref,
        bias_ref[...],
        gain_ref[...],
        own_ref,
        hidden_ref,
        slope_ref,
    )
    mid_ref[...] = output
    sums_ref[...] = edge_sums
    agg_ref[...] = agg
    pre_ref[...] = node_pre
    pool_row = pool_ref[...]
    pooled = matmul(one_hot_columns(pool_row, 0, NC_DEV), output)
    coarse = pooled / pool_counts(pool_row)
    coarse_ref[...] = coarse.astype(BF16)
    send_blocks(coarse, blocks_ref, (s0, s1, s2, s3))


def coarse_ahead(
    blocks_ref, x_ref, h0, h1, h2, h3, edges_ref, w_ref, bias_ref, gain_ref, own_ref,
    out_ref, s0, s1, s2, s3, sums_ref, agg_ref, pre_ref, slope_ref,
    extended_ref, hidden_ref,
):
    gather_halos(x_ref, (h0, h1, h2, h3), extended_ref)
    output, edge_sums, agg, node_pre = forward_step(
        x_ref[...],
        extended_ref[...],
        edges_ref[0:1, :],
        edges_ref[1:2, :],
        w_ref.at[0],
        bias_ref[0:1, :],
        gain_ref[0:1, :],
        own_ref,
        hidden_ref,
        slope_ref,
    )
    out_ref[...] = output
    sums_ref[...] = edge_sums
    agg_ref[...] = agg
    pre_ref[...] = node_pre
    send_blocks(output.astype(F32), blocks_ref, (s0, s1, s2, s3))


def put_halo_grads(grad_halo, halo_ref, out_refs):
    halo_ref[...] = grad_halo.astype(BF16)
    for group, out_ref in zip(place(), out_refs, strict=True):
        out_ref[...] = halo_ref[rows_at(group, BLOCK), :]


def coarse_turn(
    loss_scale, x_ref, h0, h1, h2, h3, edges_ref, w_ref, bias_ref, gain_ref, pool_ref, mid_ref, cot_ref,
    own_ref,
    out_ref, grad_ref, g0, g1, g2, g3, grads_ref,
    extended_ref, hidden_ref, slope_ref, act_ref, halo_ref,
):
    gather_halos(x_ref, (h0, h1, h2, h3), extended_ref)
    x = x_ref[...]
    extended = extended_ref[...]
    senders, receivers = edges_ref[0:1, :], edges_ref[1:2, :]
    gain = gain_ref[1:2, :]
    weights = w_ref.at[1]
    output, edge_sums, agg, node_pre = forward_step(
        x, extended, senders, receivers, weights, bias_ref[1:2, :], gain, own_ref, hidden_ref, slope_ref
    )
    pool_row = pool_ref[...]
    lifted = matmul(one_hot_rows(pool_row, NC_DEV), output)
    out_ref[...] = (mid_ref[...].astype(F32) + lifted).astype(BF16)
    upstream = matmul(one_hot_columns(pool_row, 0, NC_DEV), cot_ref[...]) * loss_scale
    grad_nodes, grad_halo = backward_step(
        upstream, x, extended, senders, receivers, weights, gain, edge_sums, agg, node_pre,
        slope_ref, act_ref, grads_ref, True,
    )
    grad_ref[...] = grad_nodes
    put_halo_grads(grad_halo, halo_ref, (g0, g1, g2, g3))


def add_returned(grad_ref, returned, blocks_ref, total_ref):
    total_ref[...] = grad_ref[...]
    for direction, piece in zip(place(), returned, strict=True):
        name = jnp.broadcast_to(listed(blocks_ref, direction), (BLOCK, H))
        values = piece[...].astype(F32)
        for block in range(NC_DEV // BLOCK):
            total_ref[block * BLOCK : (block + 1) * BLOCK, :] += jnp.where(name == block, values, 0.0)


def coarse_behind(
    blocks_ref, grad_in_ref, r0, r1, r2, r3, x_ref, h0, h1, h2, h3, edges_ref, w_ref, gain_ref,
    sums_ref, agg_ref, pre_ref, slope_ref,
    grad_ref, g0, g1, g2, g3, grads_ref,
    extended_ref, total_ref, act_ref, halo_ref,
):
    gather_halos(x_ref, (h0, h1, h2, h3), extended_ref)
    add_returned(grad_in_ref, (r0, r1, r2, r3), blocks_ref, total_ref)
    grad_nodes, grad_halo = backward_step(
        total_ref[...],
        x_ref[...],
        extended_ref[...],
        edges_ref[0:1, :],
        edges_ref[1:2, :],
        w_ref.at[0],
        gain_ref[0:1, :],
        sums_ref[...],
        agg_ref[...],
        pre_ref[...],
        slope_ref,
        act_ref,
        grads_ref,
        True,
    )
    grad_ref[...] = grad_nodes
    put_halo_grads(grad_halo, halo_ref, (g0, g1, g2, g3))


def fine_behind(
    loss_scale, root, live_ref, blocks_ref, grad_in_ref, r0, r1, r2, r3, x_ref, h0, h1, h2, h3, edges_ref,
    pool_ref, cot_ref, w_ref, gain_ref, sums_ref, agg_ref, pre_ref, slope_ref, grads_0_ref, grads_1_ref,
    pooled_ref, packed_ref,
    extended_ref, total_ref, act_ref, grads_ref,
):
    gather_halos(x_ref, (h0, h1, h2, h3), extended_ref)
    add_returned(grad_in_ref, (r0, r1, r2, r3), blocks_ref, total_ref)
    total = total_ref[...]
    pooled_ref[...] = total * root
    pool_row = pool_ref[...]
    shared = halves(total / pool_counts(pool_row))
    upstream = cot_ref[...].astype(F32) * loss_scale + joined(
        matmul(one_hot_rows(pool_row, NC_DEV), shared)
    )
    backward_step(
        upstream,
        x_ref[...],
        extended_ref[...],
        edges_ref[0:1, :],
        live_receivers(edges_ref, live_ref),
        w_ref,
        gain_ref[...],
        sums_ref[...],
        agg_ref[...],
        pre_ref[...],
        slope_ref,
        act_ref,
        grads_ref,
        False,
    )
    sources = (grads_ref, grads_0_ref, grads_1_ref)
    for index, source in enumerate(sources):
        packed_ref[index * 5 * H : (index + 1) * 5 * H, :] = source[0 : 5 * H, :].astype(SCATTER_WIRE)
    small = [source[5 * H :, :] for source in sources]
    small.append(jnp.zeros((PACKED - SMALL - 24, H), F32))
    packed_ref[SMALL:, :] = jnp.concatenate(small, axis=0).astype(SCATTER_WIRE)


def sum_parts(parts_ref, out_ref):
    values = [parts_ref[index].astype(F32) for index in range(parts_ref.shape[0])]
    while len(values) > 1:
        values = [a + b for a, b in zip(values[0::2], values[1::2], strict=True)]
    out_ref[...] = values[0]


def sum_and_spread(parts_ref, out_ref):
    values = [parts_ref[index].astype(F32) for index in range(parts_ref.shape[0])]
    while len(values) > 1:
        values = [a + b for a, b in zip(values[0::2], values[1::2], strict=True)]
    for index in range(out_ref.shape[0]):
        out_ref[index] = values[0]


def spread(piece_ref, out_ref):
    piece = piece_ref[...].astype(out_ref.dtype)
    for index in range(out_ref.shape[0]):
        out_ref[index] = piece


def finish(all_ref, fine_ref, coarse_ref, fb_ref, fg_ref, cb_ref, cg_ref):
    fine_ref[...] = all_ref[0 : 5 * H, :].astype(F32)
    coarse_ref[...] = all_ref[5 * H : SMALL, :].astype(F32)
    small = all_ref[SMALL : SMALL + 32, :].astype(F32)
    fb_ref[...] = small[0:1]
    fg_ref[...] = small[1:2]
    cb_ref[...] = jnp.concatenate([small[8:9], small[16:17]], axis=0)
    cg_ref[...] = jnp.concatenate([small[9:10], small[17:18]], axis=0)


def reduce_all(packed):
    across, along = lax.axis_size("gx"), lax.axis_size("gy")
    rows = PACKED // across
    part = rows // along
    pieces = lax.all_to_all(packed.reshape(across, rows, H), "gx", 0, 0)
    (mine,) = call(sum_parts, [], [pieces], [((rows, H), F32)], [])
    pieces = lax.all_to_all(mine.reshape(along, part, H), "gy", 0, 0)
    (shared,) = call(sum_and_spread, [], [pieces], [((along, part, H), F32)], [])
    mine = lax.all_to_all(shared, "gy", 0, 0).reshape(rows, H)
    (shared,) = call(spread, [], [mine], [((across, rows, H), GATHER_WIRE)], [])
    everything = lax.all_to_all(shared, "gx", 0, 0).reshape(PACKED, H)
    return call(
        finish,
        [],
        [everything],
        [((5 * H, H), F32), ((10 * H, H), F32)] + [((1, H), F32)] * 2 + [((2, H), F32)] * 2,
        [],
    )


def call(kernel, scalars, arrays, outs, scratch):
    vmem = pl.BlockSpec(memory_space=pltpu.VMEM)
    smem = pl.BlockSpec(memory_space=pltpu.SMEM)
    return pl.pallas_call(
        kernel,
        out_shape=[jax.ShapeDtypeStruct(shape, dtype) for shape, dtype in outs],
        in_specs=[smem] * len(scalars) + [vmem] * len(arrays),
        out_specs=[vmem] * len(outs),
        scratch_shapes=[pltpu.VMEM(shape, dtype) for shape, dtype in scratch],
        compiler_params=pltpu.CompilerParams(vmem_limit_bytes=SCOPED),
        cost_estimate=COST,
    )(*scalars, *arrays)


def exchange(pieces):
    received = []
    for piece, (axis, first) in zip(pieces, (("gy", 1), ("gx", 1), ("gy", 0), ("gx", 0)), strict=True):
        pairs = []
        for i in range(first, lax.axis_size(axis) - 1, 2):
            pairs += [(i, i + 1), (i + 1, i)]
        received.append(lax.ppermute(piece, axis, pairs))
    return received


def stage(*refs):
    blocks_ref, sources = refs[0], refs[1:-2]
    count = (len(sources) - 4) // 2
    sources, pieces, targets = sources[:count], sources[count : count + 4], sources[count + 4 :]
    picks_ref, semaphores = refs[-2:]
    picking = pltpu.make_async_copy(blocks_ref, picks_ref, semaphores.at[0])
    picking.start()
    copies = [
        pltpu.make_async_copy(source, target, semaphores.at[index])
        for index, (source, target) in enumerate(zip(sources, targets, strict=True), 1)
    ]
    for copy in copies:
        copy.start()
    picking.wait()
    copies[0].wait()
    for direction, piece in zip(place(), pieces, strict=True):
        piece[...] = targets[0][rows_at(picks_ref[direction], BLOCK), :]
    for copy in copies[1:]:
        copy.wait()


def staged(picks, arrays):
    hbm = pl.BlockSpec(memory_space=pltpu.HBM)
    vmem = pl.BlockSpec(memory_space=pltpu.VMEM)
    block = jax.ShapeDtypeStruct((BLOCK, H), BF16)
    outs = pl.pallas_call(
        stage,
        out_shape=[block] * 4 + [jax.ShapeDtypeStruct(a.shape, a.dtype) for a in arrays],
        in_specs=[hbm] * (1 + len(arrays)),
        out_specs=[vmem] * (4 + len(arrays)),
        scratch_shapes=[
            pltpu.SMEM(picks.shape, jnp.int32),
            pltpu.SemaphoreType.DMA((1 + len(arrays),)),
        ],
        compiler_params=pltpu.CompilerParams(vmem_limit_bytes=SCOPED),
    )(*[pltpu.with_memory_space_constraint(a, pltpu.HBM) for a in (picks, *arrays)])
    return outs[:4], outs[4:]


def body(
    fine_nodes,
    fine_edges,
    fine_live,
    fine_halo,
    pool_map,
    coarse_edges,
    coarse_halo,
    fine_weights,
    fine_bias,
    fine_gain,
    coarse_weights,
    coarse_bias,
    coarse_gain,
    cotangent,
):
    x = fine_nodes[0, 0]
    edges = fine_edges[0, 0]
    live = fine_live.reshape(1)
    pool = pool_map[0]
    coarse_list = coarse_edges[0, 0]
    blocks = coarse_halo.reshape(1, 4)
    cot = cotangent[0, 0]
    bias = fine_bias.reshape(1, H)
    gain = fine_gain.reshape(1, H)
    rows, slots, coarse_slots = x.shape[0], edges.shape[1], coarse_list.shape[1]
    total_nodes = rows * lax.axis_size("gx") * lax.axis_size("gy")
    root = math.sqrt(total_nodes)
    block = ((BLOCK, H), BF16)

    def saved(count, edge_count):
        return [
            ((count, 2 * H), BF16),
            ((count, H), BF16),
            ((count, H), F32),
            ((edge_count, H), F32),
        ]

    sends, arrays = staged(
        fine_halo.reshape(4),
        [x, edges, pool, coarse_list, blocks, fine_weights, bias, gain]
        + [coarse_weights, coarse_bias, coarse_gain, cot],
    )
    x, edges, pool, coarse_list, blocks, fine_weights, bias, gain = arrays[:8]
    coarse_weights, coarse_bias, coarse_gain, cot = arrays[8:]
    halos = exchange(sends)

    def own_of(step, values, edge_list, weights):
        outs = [((edge_list.shape[1], H), F32)]
        return list(call(functools.partial(own_part, step), [], [values, edge_list, weights], outs, []))

    own = own_of(None, x, edges, fine_weights)
    fine_out = call(
        fine_ahead,
        [live],
        [blocks, x, *halos, edges, pool, fine_weights, bias, gain, *own],
        [((rows, H), BF16), ((NC_DEV, H), BF16)] + [block] * 4 + saved(rows, slots),
        [((rows + 4 * BLOCK, H), BF16), ((slots, H), BF16)],
    )
    mid, coarse_0, sends, fine_saved = fine_out[0], fine_out[1], fine_out[2:6], fine_out[6:]
    halos_0 = exchange(sends)
    own = own_of(0, coarse_0, coarse_list, coarse_weights)
    coarse_extended = ((NC_DEV + 4 * BLOCK, H), BF16)
    halo_grads = ((4 * BLOCK, H), BF16)
    ahead = call(
        coarse_ahead,
        [],
        [blocks, coarse_0, *halos_0, coarse_list, coarse_weights, coarse_bias, coarse_gain]
        + own,
        [((NC_DEV, H), BF16)] + [block] * 4 + saved(NC_DEV, coarse_slots),
        [coarse_extended, ((coarse_slots, H), BF16)],
    )
    coarse_1, sends, coarse_saved = ahead[0], ahead[1:5], ahead[5:]
    halos_1 = exchange(sends)
    own = own_of(1, coarse_1, coarse_list, coarse_weights)
    grads = ((GRAD_ROWS, H), F32)
    turned = call(
        functools.partial(coarse_turn, 1.0 / root),
        [],
        [coarse_1, *halos_1, coarse_list, coarse_weights, coarse_bias, coarse_gain, pool, mid, cot]
        + own,
        [((rows, H), BF16), ((NC_DEV, H), F32)] + [block] * 4 + [grads],
        [coarse_extended, ((coarse_slots, H), BF16), ((coarse_slots, H), F32)]
        + [((coarse_slots, 2 * H), BF16), halo_grads],
    )
    result, grad_nodes, grad_halo, grads_1 = turned[0], turned[1], turned[2:6], turned[6]
    returned = exchange(grad_halo)
    behind = call(
        coarse_behind,
        [],
        [blocks, grad_nodes, *returned, coarse_0, *halos_0, coarse_list]
        + [coarse_weights, coarse_gain, *coarse_saved],
        [((NC_DEV, H), F32)] + [block] * 4 + [grads],
        [coarse_extended, ((NC_DEV, H), F32), ((coarse_slots, 2 * H), BF16), halo_grads],
    )
    grad_nodes, grad_halo, grads_0 = behind[0], behind[1:5], behind[5]
    returned = exchange(grad_halo)
    grad_pooled, packed = call(
        functools.partial(fine_behind, 1.0 / root, root),
        [live],
        [blocks, grad_nodes, *returned, x, *halos, edges, pool, cot, fine_weights, gain, *fine_saved]
        + [grads_0, grads_1],
        [((NC_DEV, H), F32), ((PACKED, H), SCATTER_WIRE)],
        [((rows + 4 * BLOCK, H), BF16), ((NC_DEV, H), F32), ((slots, 2 * H), BF16), grads],
    )
    fine_w, coarse_w, fine_b, fine_g, coarse_b, coarse_g = reduce_all(packed)
    return (
        result[None, None],
        fine_w.reshape(5, H, H),
        fine_b.reshape(H),
        fine_g.reshape(H),
        coarse_w.reshape(2, 5, H, H),
        coarse_b,
        coarse_g,
        grad_pooled[None, None],
    )


def solution(mesh):
    tiled = P("gx", "gy", None, None)
    return jax.shard_map(
        body,
        mesh=mesh,
        in_specs=(
            tiled,
            tiled,
            P("gx", "gy"),
            tiled,
            P("gx", "gy", None),
            tiled,
            tiled,
            P(),
            P(),
            P(),
            P(),
            P(),
            P(),
            tiled,
        ),
        out_specs=(tiled, P(), P(), P(), P(), P(), P(), tiled),
        check_vma=False,
    )
```

```python
import functools
import math

import jax
import jax.numpy as jnp
from jax import lax
from jax.experimental import pallas as pl
from jax.experimental.pallas import tpu as pltpu
from jax.sharding import PartitionSpec as P

BLOCK = 128
H = 128
COARSE_STEPS = 2
NC_DEV = 256
CHUNK = 256
GRAD_ROWS = 5 * H + 8
PACKED = 2048
SMALL = 15 * H
EPSILON = 1e-05
F32 = jnp.float32
BF16 = jnp.bfloat16
GATHER_WIRE = BF16
SCATTER_WIRE = BF16
SCOPED = 24 * 1024 * 1024
COST = pl.CostEstimate(flops=1 << 29, bytes_accessed=1 << 20, transcendentals=0)


def halves(values):
    high = values.astype(BF16)
    low = (values - high.astype(F32)).astype(BF16)
    return jnp.concatenate([high, low], axis=1)


def joined(values):
    return values[:, :H] + values[:, H:]


def matmul(left, right):
    return jnp.dot(left, right, preferred_element_type=F32)


def matmul_nt(left, right):
    return lax.dot_general(left, right, (((1,), (1,)), ((), ())), preferred_element_type=F32)


def matmul_tn(left, right):
    return lax.dot_general(left, right, (((0,), (0,)), ((), ())), preferred_element_type=F32)


def twice(weight):
    return jnp.concatenate([weight, weight], axis=1)


def column_of(row):
    pieces = []
    for start in range(0, row.shape[1], 128):
        wide = jnp.broadcast_to(row[:, start : start + 128], (128, 128))
        pieces.append(wide.T)
    return pieces[0] if len(pieces) == 1 else jnp.concatenate(pieces, axis=0)


def one_hot_rows(row, width):
    spread = column_of(row)
    spread = spread - lax.broadcasted_iota(jnp.int32, spread.shape, 1)
    spread = spread.astype(jnp.int16)
    one, zero = jnp.ones(spread.shape, BF16), jnp.zeros(spread.shape, BF16)
    tiles = [jnp.where(spread == start, one, zero) for start in range(0, width, 128)]
    return jnp.concatenate(tiles, axis=1)


def one_hot_columns(row, first, count):
    shape = (count, row.shape[1])
    wanted = jnp.broadcast_to(row - first, (128, row.shape[1]))
    spread = (wanted - lax.broadcasted_iota(jnp.int32, wanted.shape, 0)).astype(jnp.int16)
    one, zero = jnp.ones(spread.shape, BF16), jnp.zeros(spread.shape, BF16)
    return jnp.concatenate(
        [jnp.where(spread == start, one, zero) for start in range(0, count, 128)], axis=0
    )


def place():
    across, along = lax.axis_index("gx") % 2, lax.axis_index("gy") % 2
    return (across, 2 + along, 3 - along, 1 - across)


def rows_at(index, count):
    return pl.ds(pl.multiple_of(index * count, count), count)


def gather_halos(x_ref, halos, extended_ref):
    rows = x_ref.shape[0]
    extended_ref[0:rows, :] = x_ref[...]
    for group, halo in zip(place(), halos, strict=True):
        extended_ref[pl.ds(pl.multiple_of(rows + group * BLOCK, BLOCK), BLOCK), :] = halo[...]


def normalise(node_pre):
    centred = node_pre - jnp.mean(node_pre, axis=1, keepdims=True)
    spread = jnp.mean(centred * centred, axis=1, keepdims=True)
    scale = lax.rsqrt(spread + EPSILON)
    return centred * scale, scale


def own_part(step, x_ref, edges_ref, w_ref, own_ref):
    weights = w_ref if step is None else w_ref.at[step]
    x = x_ref[...]
    rows = x.shape[0]
    projected = jnp.concatenate(
        [halves(matmul(x, weights[0])), halves(matmul(x, weights[1]))], axis=0
    )
    for first in range(0, own_ref.shape[0], CHUNK):
        ends = [edges_ref[end : end + 1, first : first + CHUNK] for end in range(2)]
        marks = jnp.concatenate([one_hot_rows(end, rows) for end in ends], axis=1)
        own_ref[first : first + CHUNK, :] = joined(matmul(marks, projected))


def forward_step(x, extended, senders, receivers, weights, bias, gain, own_ref, hidden_ref, slope_ref):
    rows = x.shape[0]
    slots = senders.shape[1]
    width = extended.shape[0] - rows
    projected = halves(matmul(extended[rows:], weights[0]))
    for first in range(0, slots, CHUNK):
        marks = one_hot_rows(senders[:, first : first + CHUNK] - rows, width)
        own = own_ref[first : first + CHUNK, :]
        pre_act = joined(matmul(marks, projected)) + own + bias
        sigmoid = jax.nn.sigmoid(pre_act)
        hidden_ref[first : first + CHUNK, :] = (pre_act * sigmoid).astype(BF16)
        slope_ref[first : first + CHUNK, :] = sigmoid * (1.0 + pre_act * (1.0 - sigmoid))
    hidden = hidden_ref[...]
    gathered = jnp.concatenate(
        [
            matmul(one_hot_columns(receivers, first, CHUNK), hidden)
            for first in range(0, rows, CHUNK)
        ],
        axis=0,
    )
    edge_sums = halves(gathered)
    agg = matmul(edge_sums, jnp.concatenate([weights[2], weights[2]], axis=0)).astype(BF16)
    both = jnp.concatenate([x, agg], axis=1)
    node_pre = matmul(both, jnp.concatenate([weights[3], weights[4]], axis=0))
    normed, _ = normalise(node_pre)
    output = (x.astype(F32) + gain * normed).astype(BF16)
    return output, edge_sums, agg, node_pre


def backward_step(
    upstream,
    x,
    extended,
    senders,
    receivers,
    weights,
    gain,
    edge_sums,
    agg,
    node_pre,
    slope_ref,
    act_ref,
    grads_ref,
    want_input,
):
    rows = x.shape[0]
    slots = senders.shape[1]
    normed, scale = normalise(node_pre)
    grad_gain = jnp.sum(upstream * normed, axis=0, keepdims=True)
    seed = upstream * gain
    grad_pre = scale * (
        seed
        - jnp.mean(seed, axis=1, keepdims=True)
        - normed * jnp.mean(seed * normed, axis=1, keepdims=True)
    )
    pre_parts = halves(grad_pre)
    both = jnp.concatenate([x, agg], axis=1)
    terms = joined(matmul_tn(both, pre_parts))
    grads_ref[3 * H : 5 * H, :] = terms
    back = matmul_nt(pre_parts, jnp.concatenate([twice(weights[4]), twice(weights[3])], axis=0))
    agg_parts = halves(back[:, :H])
    quads = matmul_tn(edge_sums, agg_parts)
    grads_ref[2 * H : 3 * H, :] = joined(quads[:H] + quads[H:])
    message_parts = halves(matmul_nt(agg_parts, twice(weights[2])))
    for first in range(0, slots, CHUNK):
        marks = one_hot_rows(receivers[:, first : first + CHUNK], rows)
        grad_act = joined(matmul(marks, message_parts)) * slope_ref[first : first + CHUNK, :]
        act_ref[first : first + CHUNK, :] = halves(grad_act)
    act = act_ref[...]
    width = extended.shape[0]
    send_parts = halves(
        jnp.concatenate(
            [
                joined(matmul(one_hot_columns(senders, first, CHUNK), act))
                for first in range(0, width, CHUNK)
            ],
            axis=0,
        )
    )
    grad_recv = jnp.concatenate(
        [
            joined(matmul(one_hot_columns(receivers, first, CHUNK), act))
            for first in range(0, rows, CHUNK)
        ],
        axis=0,
    )
    recv_parts = halves(grad_recv)
    grads_ref[0:H, :] = joined(matmul_tn(extended, send_parts))
    grads_ref[H : 2 * H, :] = joined(matmul_tn(x, recv_parts))
    grad_bias = jnp.sum(grad_recv, axis=0, keepdims=True)
    grads_ref[5 * H :, :] = jnp.concatenate(
        [grad_bias, grad_gain, jnp.zeros((GRAD_ROWS - 5 * H - 2, H), F32)], axis=0
    )
    if not want_input:
        return None, None
    grad_ext = matmul_nt(send_parts, twice(weights[0]))
    grad_nodes = (
        upstream + back[:, H:] + matmul_nt(recv_parts, twice(weights[1])) + grad_ext[:rows]
    )
    return grad_nodes, grad_ext[rows:]


def pool_counts(pool_row):
    shape = (NC_DEV, pool_row.shape[1])
    marks = lax.broadcasted_iota(jnp.int32, shape, 0) == jnp.broadcast_to(pool_row, shape)
    return jnp.sum(jnp.where(marks, 1.0, 0.0), axis=1, keepdims=True)


def listed(blocks_ref, direction):
    blocks = blocks_ref[...]
    chosen = lax.broadcasted_iota(jnp.int32, blocks.shape, 1) == direction
    return jnp.sum(jnp.where(chosen, blocks, 0), axis=1, keepdims=True)


def send_blocks(values, blocks_ref, out_refs):
    for direction, out_ref in zip(place(), out_refs, strict=True):
        name = jnp.broadcast_to(listed(blocks_ref, direction), (BLOCK, H))
        piece = values[:BLOCK]
        for block in range(1, NC_DEV // BLOCK):
            piece = jnp.where(name == block, values[block * BLOCK : (block + 1) * BLOCK], piece)
        out_ref[...] = piece.astype(BF16)


def live_receivers(edges_ref, live_ref):
    receivers = edges_ref[1:2, :]
    slot = lax.broadcasted_iota(jnp.int32, receivers.shape, 1)
    return jnp.where(slot < live_ref[0], receivers, -1)


def fine_ahead(
    live_ref, blocks_ref, x_ref, h0, h1, h2, h3, edges_ref, pool_ref, w_ref, bias_ref, gain_ref, own_ref,
    mid_ref, coarse_ref, s0, s1, s2, s3, sums_ref, agg_ref, pre_ref, slope_ref,
    extended_ref, hidden_ref,
):
    gather_halos(x_ref, (h0, h1, h2, h3), extended_ref)
    output, edge_sums, agg, node_pre = forward_step(
        x_ref[...],
        extended_ref[...],
        edges_ref[0:1, :],
        live_receivers(edges_ref, live_ref),
        w_ref,
        bias_ref[...],
        gain_ref[...],
        own_ref,
        hidden_ref,
        slope_ref,
    )
    mid_ref[...] = output
    sums_ref[...] = edge_sums
    agg_ref[...] = agg
    pre_ref[...] = node_pre
    pool_row = pool_ref[...]
    pooled = matmul(one_hot_columns(pool_row, 0, NC_DEV), output)
    coarse = pooled / pool_counts(pool_row)
    coarse_ref[...] = coarse.astype(BF16)
    send_blocks(coarse, blocks_ref, (s0, s1, s2, s3))


def coarse_ahead(
    blocks_ref, x_ref, h0, h1, h2, h3, edges_ref, w_ref, bias_ref, gain_ref, own_ref,
    out_ref, s0, s1, s2, s3, sums_ref, agg_ref, pre_ref, slope_ref,
    extended_ref, hidden_ref,
):
    gather_halos(x_ref, (h0, h1, h2, h3), extended_ref)
    output, edge_sums, agg, node_pre = forward_step(
        x_ref[...],
        extended_ref[...],
        edges_ref[0:1, :],
        edges_ref[1:2, :],
        w_ref.at[0],
        bias_ref[0:1, :],
        gain_ref[0:1, :],
        own_ref,
        hidden_ref,
        slope_ref,
    )
    out_ref[...] = output
    sums_ref[...] = edge_sums
    agg_ref[...] = agg
    pre_ref[...] = node_pre
    send_blocks(output.astype(F32), blocks_ref, (s0, s1, s2, s3))


def put_halo_grads(grad_halo, halo_ref, out_refs):
    halo_ref[...] = grad_halo.astype(BF16)
    for group, out_ref in zip(place(), out_refs, strict=True):
        out_ref[...] = halo_ref[rows_at(group, BLOCK), :]


def coarse_turn(
    loss_scale, x_ref, h0, h1, h2, h3, edges_ref, w_ref, bias_ref, gain_ref, pool_ref, mid_ref, cot_ref,
    own_ref,
    out_ref, grad_ref, g0, g1, g2, g3, grads_ref,
    extended_ref, hidden_ref, slope_ref, act_ref, halo_ref,
):
    gather_halos(x_ref, (h0, h1, h2, h3), extended_ref)
    x = x_ref[...]
    extended = extended_ref[...]
    senders, receivers = edges_ref[0:1, :], edges_ref[1:2, :]
    gain = gain_ref[1:2, :]
    weights = w_ref.at[1]
    output, edge_sums, agg, node_pre = forward_step(
        x, extended, senders, receivers, weights, bias_ref[1:2, :], gain, own_ref, hidden_ref, slope_ref
    )
    pool_row = pool_ref[...]
    lifted = matmul(one_hot_rows(pool_row, NC_DEV), output)
    out_ref[...] = (mid_ref[...].astype(F32) + lifted).astype(BF16)
    upstream = matmul(one_hot_columns(pool_row, 0, NC_DEV), cot_ref[...]) * loss_scale
    grad_nodes, grad_halo = backward_step(
        upstream, x, extended, senders, receivers, weights, gain, edge_sums, agg, node_pre,
        slope_ref, act_ref, grads_ref, True,
    )
    grad_ref[...] = grad_nodes
    put_halo_grads(grad_halo, halo_ref, (g0, g1, g2, g3))


def add_returned(grad_ref, returned, blocks_ref, total_ref):
    total_ref[...] = grad_ref[...]
    for direction, piece in zip(place(), returned, strict=True):
        name = jnp.broadcast_to(listed(blocks_ref, direction), (BLOCK, H))
        values = piece[...].astype(F32)
        for block in range(NC_DEV // BLOCK):
            total_ref[block * BLOCK : (block + 1) * BLOCK, :] += jnp.where(name == block, values, 0.0)


def coarse_behind(
    blocks_ref, grad_in_ref, r0, r1, r2, r3, x_ref, h0, h1, h2, h3, edges_ref, w_ref, gain_ref,
    sums_ref, agg_ref, pre_ref, slope_ref,
    grad_ref, g0, g1, g2, g3, grads_ref,
    extended_ref, total_ref, act_ref, halo_ref,
):
    gather_halos(x_ref, (h0, h1, h2, h3), extended_ref)
    add_returned(grad_in_ref, (r0, r1, r2, r3), blocks_ref, total_ref)
    grad_nodes, grad_halo = backward_step(
        total_ref[...],
        x_ref[...],
        extended_ref[...],
        edges_ref[0:1, :],
        edges_ref[1:2, :],
        w_ref.at[0],
        gain_ref[0:1, :],
        sums_ref[...],
        agg_ref[...],
        pre_ref[...],
        slope_ref,
        act_ref,
        grads_ref,
        True,
    )
    grad_ref[...] = grad_nodes
    put_halo_grads(grad_halo, halo_ref, (g0, g1, g2, g3))


def fine_behind(
    loss_scale, root, live_ref, blocks_ref, grad_in_ref, r0, r1, r2, r3, x_ref, h0, h1, h2, h3, edges_ref,
    pool_ref, cot_ref, w_ref, gain_ref, sums_ref, agg_ref, pre_ref, slope_ref, grads_0_ref, grads_1_ref,
    pooled_ref, packed_ref,
    extended_ref, total_ref, act_ref, grads_ref,
):
    gather_halos(x_ref, (h0, h1, h2, h3), extended_ref)
    add_returned(grad_in_ref, (r0, r1, r2, r3), blocks_ref, total_ref)
    total = total_ref[...]
    pooled_ref[...] = total * root
    pool_row = pool_ref[...]
    shared = halves(total / pool_counts(pool_row))
    upstream = cot_ref[...].astype(F32) * loss_scale + joined(
        matmul(one_hot_rows(pool_row, NC_DEV), shared)
    )
    backward_step(
        upstream,
        x_ref[...],
        extended_ref[...],
        edges_ref[0:1, :],
        live_receivers(edges_ref, live_ref),
        w_ref,
        gain_ref[...],
        sums_ref[...],
        agg_ref[...],
        pre_ref[...],
        slope_ref,
        act_ref,
        grads_ref,
        False,
    )
    sources = (grads_ref, grads_0_ref, grads_1_ref)
    for index, source in enumerate(sources):
        packed_ref[index * 5 * H : (index + 1) * 5 * H, :] = source[0 : 5 * H, :].astype(SCATTER_WIRE)
    small = [source[5 * H :, :] for source in sources]
    small.append(jnp.zeros((PACKED - SMALL - 24, H), F32))
    packed_ref[SMALL:, :] = jnp.concatenate(small, axis=0).astype(SCATTER_WIRE)


def sum_parts(parts_ref, out_ref):
    values = [parts_ref[index].astype(F32) for index in range(parts_ref.shape[0])]
    while len(values) > 1:
        values = [a + b for a, b in zip(values[0::2], values[1::2], strict=True)]
    out_ref[...] = values[0]


def sum_and_spread(parts_ref, out_ref):
    values = [parts_ref[index].astype(F32) for index in range(parts_ref.shape[0])]
    while len(values) > 1:
        values = [a + b for a, b in zip(values[0::2], values[1::2], strict=True)]
    for index in range(out_ref.shape[0]):
        out_ref[index] = values[0]


def spread(piece_ref, out_ref):
    piece = piece_ref[...].astype(out_ref.dtype)
    for index in range(out_ref.shape[0]):
        out_ref[index] = piece


def finish(all_ref, fine_ref, coarse_ref, fb_ref, fg_ref, cb_ref, cg_ref):
    fine_ref[...] = all_ref[0 : 5 * H, :].astype(F32)
    coarse_ref[...] = all_ref[5 * H : SMALL, :].astype(F32)
    small = all_ref[SMALL : SMALL + 32, :].astype(F32)
    fb_ref[...] = small[0:1]
    fg_ref[...] = small[1:2]
    cb_ref[...] = jnp.concatenate([small[8:9], small[16:17]], axis=0)
    cg_ref[...] = jnp.concatenate([small[9:10], small[17:18]], axis=0)


def reduce_all(packed):
    across, along = lax.axis_size("gx"), lax.axis_size("gy")
    rows = PACKED // across
    part = rows // along
    pieces = lax.all_to_all(packed.reshape(across, rows, H), "gx", 0, 0)
    (mine,) = call(sum_parts, [], [pieces], [((rows, H), F32)], [])
    pieces = lax.all_to_all(mine.reshape(along, part, H), "gy", 0, 0)
    (shared,) = call(sum_and_spread, [], [pieces], [((along, part, H), F32)], [])
    mine = lax.all_to_all(shared, "gy", 0, 0).reshape(rows, H)
    (shared,) = call(spread, [], [mine], [((across, rows, H), GATHER_WIRE)], [])
    everything = lax.all_to_all(shared, "gx", 0, 0).reshape(PACKED, H)
    return call(
        finish,
        [],
        [everything],
        [((5 * H, H), F32), ((10 * H, H), F32)] + [((1, H), F32)] * 2 + [((2, H), F32)] * 2,
        [],
    )


def call(kernel, scalars, arrays, outs, scratch):
    vmem = pl.BlockSpec(memory_space=pltpu.VMEM)
    smem = pl.BlockSpec(memory_space=pltpu.SMEM)
    return pl.pallas_call(
        kernel,
        out_shape=[jax.ShapeDtypeStruct(shape, dtype) for shape, dtype in outs],
        in_specs=[smem] * len(scalars) + [vmem] * len(arrays),
        out_specs=[vmem] * len(outs),
        scratch_shapes=[pltpu.VMEM(shape, dtype) for shape, dtype in scratch],
        compiler_params=pltpu.CompilerParams(vmem_limit_bytes=SCOPED),
        cost_estimate=COST,
    )(*scalars, *arrays)


def exchange(pieces):
    received = []
    for piece, (axis, first) in zip(pieces, (("gx", 1), ("gy", 1), ("gy", 0), ("gx", 0)), strict=True):
        pairs = []
        for i in range(first, lax.axis_size(axis) - 1, 2):
            pairs += [(i, i + 1), (i + 1, i)]
        received.append(lax.ppermute(piece, axis, pairs))
    return received


def stage(*refs):
    blocks_ref, sources = refs[0], refs[1:-2]
    count = (len(sources) - 4) // 2
    sources, pieces, targets = sources[:count], sources[count : count + 4], sources[count + 4 :]
    picks_ref, semaphores = refs[-2:]
    picking = pltpu.make_async_copy(blocks_ref, picks_ref, semaphores.at[0])
    picking.start()
    copies = [
        pltpu.make_async_copy(source, target, semaphores.at[index])
        for index, (source, target) in enumerate(zip(sources, targets, strict=True), 1)
    ]
    for copy in copies:
        copy.start()
    picking.wait()
    copies[0].wait()
    for direction, piece in zip(place(), pieces, strict=True):
        piece[...] = targets[0][rows_at(picks_ref[direction], BLOCK), :]
    for copy in copies[1:]:
        copy.wait()


def staged(picks, arrays):
    hbm = pl.BlockSpec(memory_space=pltpu.HBM)
    vmem = pl.BlockSpec(memory_space=pltpu.VMEM)
    block = jax.ShapeDtypeStruct((BLOCK, H), BF16)
    outs = pl.pallas_call(
        stage,
        out_shape=[block] * 4 + [jax.ShapeDtypeStruct(a.shape, a.dtype) for a in arrays],
        in_specs=[hbm] * (1 + len(arrays)),
        out_specs=[vmem] * (4 + len(arrays)),
        scratch_shapes=[
            pltpu.SMEM(picks.shape, jnp.int32),
            pltpu.SemaphoreType.DMA((1 + len(arrays),)),
        ],
        compiler_params=pltpu.CompilerParams(vmem_limit_bytes=SCOPED),
    )(*[pltpu.with_memory_space_constraint(a, pltpu.HBM) for a in (picks, *arrays)])
    return outs[:4], outs[4:]


def body(
    fine_nodes,
    fine_edges,
    fine_live,
    fine_halo,
    pool_map,
    coarse_edges,
    coarse_halo,
    fine_weights,
    fine_bias,
    fine_gain,
    coarse_weights,
    coarse_bias,
    coarse_gain,
    cotangent,
):
    x = fine_nodes[0, 0]
    edges = fine_edges[0, 0]
    live = fine_live.reshape(1)
    pool = pool_map[0]
    coarse_list = coarse_edges[0, 0]
    blocks = coarse_halo.reshape(1, 4)
    cot = cotangent[0, 0]
    bias = fine_bias.reshape(1, H)
    gain = fine_gain.reshape(1, H)
    rows, slots, coarse_slots = x.shape[0], edges.shape[1], coarse_list.shape[1]
    total_nodes = rows * lax.axis_size("gx") * lax.axis_size("gy")
    root = math.sqrt(total_nodes)
    block = ((BLOCK, H), BF16)

    def saved(count, edge_count):
        return [
            ((count, 2 * H), BF16),
            ((count, H), BF16),
            ((count, H), F32),
            ((edge_count, H), F32),
        ]

    sends, arrays = staged(
        fine_halo.reshape(4),
        [x, edges, pool, coarse_list, blocks, fine_weights, bias, gain]
        + [coarse_weights, coarse_bias, coarse_gain, cot],
    )
    x, edges, pool, coarse_list, blocks, fine_weights, bias, gain = arrays[:8]
    coarse_weights, coarse_bias, coarse_gain, cot = arrays[8:]
    halos = exchange(sends)

    def own_of(step, values, edge_list, weights):
        outs = [((edge_list.shape[1], H), F32)]
        return list(call(functools.partial(own_part, step), [], [values, edge_list, weights], outs, []))

    own = own_of(None, x, edges, fine_weights)
    fine_out = call(
        fine_ahead,
        [live],
        [blocks, x, *halos, edges, pool, fine_weights, bias, gain, *own],
        [((rows, H), BF16), ((NC_DEV, H), BF16)] + [block] * 4 + saved(rows, slots),
        [((rows + 4 * BLOCK, H), BF16), ((slots, H), BF16)],
    )
    mid, coarse_0, sends, fine_saved = fine_out[0], fine_out[1], fine_out[2:6], fine_out[6:]
    halos_0 = exchange(sends)
    own = own_of(0, coarse_0, coarse_list, coarse_weights)
    coarse_extended = ((NC_DEV + 4 * BLOCK, H), BF16)
    halo_grads = ((4 * BLOCK, H), BF16)
    ahead = call(
        coarse_ahead,
        [],
        [blocks, coarse_0, *halos_0, coarse_list, coarse_weights, coarse_bias, coarse_gain]
        + own,
        [((NC_DEV, H), BF16)] + [block] * 4 + saved(NC_DEV, coarse_slots),
        [coarse_extended, ((coarse_slots, H), BF16)],
    )
    coarse_1, sends, coarse_saved = ahead[0], ahead[1:5], ahead[5:]
    halos_1 = exchange(sends)
    own = own_of(1, coarse_1, coarse_list, coarse_weights)
    grads = ((GRAD_ROWS, H), F32)
    turned = call(
        functools.partial(coarse_turn, 1.0 / root),
        [],
        [coarse_1, *halos_1, coarse_list, coarse_weights, coarse_bias, coarse_gain, pool, mid, cot]
        + own,
        [((rows, H), BF16), ((NC_DEV, H), F32)] + [block] * 4 + [grads],
        [coarse_extended, ((coarse_slots, H), BF16), ((coarse_slots, H), F32)]
        + [((coarse_slots, 2 * H), BF16), halo_grads],
    )
    result, grad_nodes, grad_halo, grads_1 = turned[0], turned[1], turned[2:6], turned[6]
    returned = exchange(grad_halo)
    behind = call(
        coarse_behind,
        [],
        [blocks, grad_nodes, *returned, coarse_0, *halos_0, coarse_list]
        + [coarse_weights, coarse_gain, *coarse_saved],
        [((NC_DEV, H), F32)] + [block] * 4 + [grads],
        [coarse_extended, ((NC_DEV, H), F32), ((coarse_slots, 2 * H), BF16), halo_grads],
    )
    grad_nodes, grad_halo, grads_0 = behind[0], behind[1:5], behind[5]
    returned = exchange(grad_halo)
    grad_pooled, packed = call(
        functools.partial(fine_behind, 1.0 / root, root),
        [live],
        [blocks, grad_nodes, *returned, x, *halos, edges, pool, cot, fine_weights, gain, *fine_saved]
        + [grads_0, grads_1],
        [((NC_DEV, H), F32), ((PACKED, H), SCATTER_WIRE)],
        [((rows + 4 * BLOCK, H), BF16), ((NC_DEV, H), F32), ((slots, 2 * H), BF16), grads],
    )
    fine_w, coarse_w, fine_b, fine_g, coarse_b, coarse_g = reduce_all(packed)
    return (
        result[None, None],
        fine_w.reshape(5, H, H),
        fine_b.reshape(H),
        fine_g.reshape(H),
        coarse_w.reshape(2, 5, H, H),
        coarse_b,
        coarse_g,
        grad_pooled[None, None],
    )


def solution(mesh):
    tiled = P("gx", "gy", None, None)
    return jax.shard_map(
        body,
        mesh=mesh,
        in_specs=(
            tiled,
            tiled,
            P("gx", "gy"),
            tiled,
            P("gx", "gy", None),
            tiled,
            tiled,
            P(),
            P(),
            P(),
            P(),
            P(),
            P(),
            tiled,
        ),
        out_specs=(tiled, P(), P(), P(), P(), P(), P(), tiled),
        check_vma=False,
    )
```
